128 devices in a mesh: seq: 8 (over x, y_lo), tensor: 16 (over z, y_hi, core).
Axes of the slice: x: 4, y: 4 (y_hi: 2, y_lo: 2; y = y_hi * 2 + y_lo), z: 4, core: 2. Of those that a mesh axis runs over, the one named last changes fastest.
Arguments:
- inputs: bfloat16 [2048, 12288], P(('seq', 'tensor')), may hold values from -6 to 6
- out_grad: bfloat16 [2048, 12288], P(('seq', 'tensor')), may hold values from -0.59765625 to 0.59765625
- hidden_pre: bfloat16 [2048, 24576], P('seq', 'tensor'), may hold values from -8 to 8
- first_blocks: bfloat16 [4608, 128, 128], P('tensor'), may hold values from -0.078125 to 0.078125
- first_feat: int32 [4608], P('tensor'), may hold values from 0 to 95
- first_hid: int32 [4608], P('tensor'), may hold values from 0 to 191, as said below
- first_live: int32 [16], P('tensor'), may hold values from 144 to 288, as said below
- second_blocks: bfloat16 [4608, 128, 128], P('tensor'), may hold values from -0.109375 to 0.109375
- second_feat: int32 [4608], P('tensor'), may hold values from 0 to 95
- second_hid: int32 [4608], P('tensor'), may hold values from 0 to 191, as said below
- second_live: int32 [16], P('tensor'), may hold values from 144 to 288, as said below
Outputs:
- input_grad: bfloat16 [2048, 12288], P(('seq', 'tensor'))
- first_grad: bfloat16 [4608, 128, 128], P('tensor', 'seq')
- second_grad: bfloat16 [4608, 128, 128], P('tensor', 'seq')
The draws below stay inside these ranges and needn't reach their ends.
Inputs may be any that keep to these rules, and one draw needn't show every extreme that they name: `first_hid`: slots of tensor index j name distinct block positions, with hidden blocks from j * 12 to (j + 1) * 12 - 1. `second_hid`: slots of tensor index j name distinct block positions, with hidden blocks from j * 12 to (j + 1) * 12 - 1. `first_live`: some index has all 288 slots live. `second_live`: some index has all 288 slots live.
All inputs are finite; a program needn't handle non-finite values.
Results may differ from the reference program's by a relative error of at most 0.023.
Values may be sent and summed in bfloat16 or wider, within the bound.
A program may use at most 256 MiB of HBM per device.

```python
import jax
import jax.numpy as jnp
from jax import lax

D = 12288
F = 24576
BLK = 128
TOKENS = 2048
NB_DEV = 288
NBLK = 4608
N_SEQ = 8
N_TENSOR = 16


def mask_positions(key, offset_seed):
    key = jax.random.fold_in(key, offset_seed)
    per_device = F // BLK // N_TENSOR
    cells = D // BLK * per_device
    device_keys = jax.random.split(key, N_TENSOR)
    chosen = jax.vmap(lambda subkey: jax.random.permutation(subkey, cells)[:NB_DEV])(device_keys)
    device_rows = jnp.arange(N_TENSOR, dtype=jnp.int32)[:, None]
    feature_idx = (chosen // per_device).astype(jnp.int32).reshape(-1)
    hidden_idx = (chosen % per_device + device_rows * per_device).astype(jnp.int32).reshape(-1)
    return (feature_idx, hidden_idx)


def live_counts(key):
    first_key, second_key = jax.random.split(key)
    counts = jax.random.randint(first_key, (N_TENSOR,), max(1, NB_DEV // 2), NB_DEV + 1)
    fullest = jax.random.randint(second_key, (), 0, N_TENSOR)
    return jnp.where(jnp.arange(N_TENSOR) == fullest, NB_DEV, counts).astype(jnp.int32)


def draw_first_feat(key, part):
    return mask_positions(key, 101)[0]


def draw_first_hid(key, part):
    return mask_positions(key, 101)[1]


def draw_second_feat(key, part):
    return mask_positions(key, 202)[0]


def draw_second_hid(key, part):
    return mask_positions(key, 202)[1]


def draw_first_live(key, part):
    key = jax.random.fold_in(key, 7)
    return live_counts(key)


def draw_second_live(key, part):
    key = jax.random.fold_in(key, 9)
    return live_counts(key)


def steps_of(key, dims, cuts, smallest, largest):
    def one(dim, parts):
        heights = jax.random.uniform(jax.random.fold_in(jax.random.fold_in(key, 6), dim), (parts,), jnp.float32, smallest / len(cuts), largest / len(cuts))
        return jnp.repeat(jnp.exp(heights), dims[dim] // parts).reshape((-1,) + (1,) * (len(dims) - dim - 1))

    loudness = one(*cuts[0])
    for cut in cuts[1:]:
        loudness = loudness * one(*cut)
    return loudness


def centred(own_key, extent, deviation, limit, shards=(), kind=jnp.bfloat16):
    loudness = steps_of(own_key, extent, shards, -0.22, 0.18) if shards else 1.0
    values = jax.random.normal(own_key, extent, jnp.float32) * deviation * loudness
    return jnp.minimum(jnp.maximum(values, -limit), limit).astype(kind)


def setup_inputs(seed: int = 0) -> dict:
    key_list = jax.random.split(jax.random.key(seed), 12)
    inputs = centred(key_list[0], (TOKENS, D), 1.0, 6.0, ((0, 128),))
    out_grad = centred(key_list[1], (TOKENS, D), 0.1, 0.59765625, ((0, 128),))
    hidden_pre = centred(key_list[2], (TOKENS, F), 1.5, 8.0, ((0, 8), (1, 16)))
    first_blocks = centred(key_list[3], (NBLK, BLK, BLK), (F // 4) ** -0.5, 0.078125, ((0, 16),))
    first_feat = draw_first_feat(jax.random.fold_in(key_list[11], 71), 0)
    first_hid = draw_first_hid(jax.random.fold_in(key_list[11], 71), 0)
    first_live = draw_first_live(jax.random.fold_in(key_list[11], 71), 0)
    second_blocks = centred(key_list[7], (NBLK, BLK, BLK), (D // 4) ** -0.5, 0.109375, ((0, 16),))
    second_feat = draw_second_feat(jax.random.fold_in(key_list[11], 71), 0)
    second_hid = draw_second_hid(jax.random.fold_in(key_list[11], 71), 0)
    second_live = draw_second_live(jax.random.fold_in(key_list[11], 71), 0)
    return {"inputs": inputs, "out_grad": out_grad, "hidden_pre": hidden_pre, "first_blocks": first_blocks, "first_feat": first_feat, "first_hid": first_hid, "first_live": first_live, "second_blocks": second_blocks, "second_feat": second_feat, "second_hid": second_hid, "second_live": second_live}


slope_coef = 0.7978845608028654
cubic_coef = 0.044715


def gelu_pair(values):
    inner_arg = slope_coef * (values + cubic_coef * values * values * values)
    tanh_part = jnp.tanh(inner_arg)
    output = 0.5 * values * (1.0 + tanh_part)
    slopes = 0.5 * (1.0 + tanh_part) + 0.5 * values * (1.0 - tanh_part * tanh_part) * slope_coef * (1.0 + 3.0 * cubic_coef * values * values)
    return output, slopes


def round_keep(values):
    return lax.optimization_barrier(values.astype(jnp.bfloat16)).astype(jnp.float32)


def reference(inputs, out_grad, hidden_pre, first_blocks, first_feat, first_hid, first_live, second_blocks, second_feat, second_hid, second_live):
    block_size = first_blocks.shape[1]
    tokens = inputs.shape[0]
    feat_count = inputs.shape[1] // block_size
    hid_count = hidden_pre.shape[1] // block_size // N_TENSOR
    slots = first_blocks.shape[0] // N_TENSOR
    in_tiles = inputs.astype(jnp.float32).reshape(tokens, feat_count, block_size)
    grad_tiles = out_grad.astype(jnp.float32).reshape(tokens, feat_count, block_size)
    hidden_ids = jnp.arange(hid_count, dtype=jnp.int32)
    feature_ids = jnp.arange(feat_count, dtype=jnp.int32)
    slot_order = jnp.arange(slots, dtype=jnp.int32)

    def group_sum(left_cols, right_cols):
        left_cols = left_cols.reshape(N_SEQ, tokens // N_SEQ, slots, block_size)
        right_cols = right_cols.reshape(N_SEQ, tokens // N_SEQ, slots, block_size)
        partial_value = jnp.einsum("stbx,stby->sbxy", left_cols, right_cols)
        return jnp.sum(round_keep(partial_value), axis=0)

    def per_device(running, device_index):
        first_slot = device_index * slots

        def device_cut(array):
            return lax.dynamic_slice_in_dim(array, first_slot, slots, 0)

        blocks_one = device_cut(first_blocks).astype(jnp.float32)
        blocks_two = device_cut(second_blocks).astype(jnp.float32)
        feat_one = device_cut(first_feat)
        feat_two = device_cut(second_feat)
        hid_one = device_cut(first_hid) - device_index * hid_count
        hid_two = device_cut(second_hid) - device_index * hid_count
        alive_one = slot_order < first_live[device_index]
        alive_two = slot_order < second_live[device_index]
        pre = lax.dynamic_slice_in_dim(hidden_pre, device_index * hid_count * block_size, hid_count * block_size, 1).astype(jnp.float32)
        values, slopes = gelu_pair(pre)
        activation = round_keep(values).reshape(tokens, hid_count, block_size)
        grad_cols = jnp.take(grad_tiles, feat_two, axis=1)
        contrib = jnp.einsum("tbf,bhf->tbh", grad_cols, blocks_two)
        onehot_two = ((hid_two[:, None] == hidden_ids[None, :]) & alive_two[:, None]).astype(jnp.float32)
        act_grad = jnp.einsum("tbh,bk->tkh", contrib, onehot_two, precision=lax.Precision.HIGHEST).reshape(tokens, hid_count * block_size)
        pre_grad = round_keep(act_grad * slopes).reshape(tokens, hid_count, block_size)
        pre_cols = jnp.take(pre_grad, hid_one, axis=1)
        back = jnp.einsum("tbh,bfh->tbf", pre_cols, blocks_one)
        onehot_one = ((feat_one[:, None] == feature_ids[None, :]) & alive_one[:, None]).astype(jnp.float32)
        input_part = jnp.einsum("tbf,bk->tkf", back, onehot_one, precision=lax.Precision.HIGHEST).reshape(tokens, feat_count * block_size)
        in_cols = jnp.take(in_tiles, feat_one, axis=1)
        act_cols = jnp.take(activation, hid_two, axis=1)
        grad_one = jnp.where(alive_one[:, None, None], group_sum(in_cols, pre_cols), 0.0).astype(jnp.bfloat16)
        grad_two = jnp.where(alive_two[:, None, None], group_sum(act_cols, grad_cols), 0.0).astype(jnp.bfloat16)
        return running + input_part, (grad_one, grad_two)

    start_sum = jnp.zeros((tokens, feat_count * block_size), jnp.float32)
    input_sum, grads = lax.scan(per_device, start_sum, jnp.arange(N_TENSOR, dtype=jnp.int32))
    first_grad = grads[0].reshape(N_TENSOR * slots, block_size, block_size)
    second_grad = grads[1].reshape(N_TENSOR * slots, block_size, block_size)
    return input_sum.astype(jnp.bfloat16), first_grad, second_grad
```

```python
import functools

import jax
import jax.numpy as jnp
from jax import lax
from jax.experimental import pallas as pl
from jax.experimental.pallas import tpu as pltpu
from jax.sharding import PartitionSpec as P

MESH = pl.DeviceIdType.MESH
BF = jnp.bfloat16
F32 = jnp.float32
ANY = pl.BlockSpec(memory_space=pl.ANY)
SMEM = pl.BlockSpec(memory_space=pltpu.SMEM)
VMEM = pl.BlockSpec(memory_space=pltpu.VMEM)
MIB = 1024 * 1024

slope_coef = 0.7978845608028654
cubic_coef = 0.044715


def gelu_value(p):
    th = jnp.tanh(slope_coef * (p + cubic_coef * p * p * p))
    return 0.5 * p * (1.0 + th)


def gelu_slope(p):
    th = jnp.tanh(slope_coef * (p + cubic_coef * p * p * p))
    return 0.5 * (1.0 + th) + 0.5 * p * (1.0 - th * th) * slope_coef * (1.0 + 3.0 * cubic_coef * p * p)


class Here:
    def __init__(self):
        s = lax.axis_index("seq")
        t = lax.axis_index("tensor")
        self.s, self.t = s, t
        self.x, self.yl = s // 2, s % 2
        self.z, self.yh, self.c = t // 4, (t // 2) % 2, t % 2

    def dev(self, dx=0, fl=0, dz=0, fh=0, fc=0):
        x = (self.x + dx) % 4
        z = (self.z + dz) % 4
        yl = (self.yl + fl) % 2
        yh = (self.yh + fh) % 2
        c = (self.c + fc) % 2
        return (x * 2 + yl, z * 4 + yh * 2 + c)


class Copies:
    def __init__(self, send, recv):
        self.send_sems, self.recv_sems = send, recv
        self.sent = []

    def send(self, i, src, dst, device):
        copy = pltpu.make_async_remote_copy(
            src_ref=src,
            dst_ref=dst,
            send_sem=self.send_sems.at[i],
            recv_sem=self.recv_sems.at[i],
            device_id=device,
            device_id_type=MESH,
        )
        copy.start()
        self.sent.append(copy)

    def arrived(self, i, dst, device):
        pltpu.make_async_remote_copy(
            src_ref=dst,
            dst_ref=dst,
            send_sem=self.send_sems.at[i],
            recv_sem=self.recv_sems.at[i],
            device_id=device,
            device_id_type=MESH,
        ).wait_recv()

    def drain(self):
        for copy in self.sent:
            copy.wait_send()


def greet(devices):
    barrier = pltpu.get_barrier_semaphore()
    for device in devices:
        pl.semaphore_signal(barrier, inc=1, device_id=device, device_id_type=MESH)
    pl.semaphore_wait(barrier, len(devices))


class TensorGather:
    def __init__(self, me, copies, base, own, slot):
        self.me, self.k, self.b, self.own, self.slot = me, copies, base, own, slot

    def at(self, dz, fh, fc=0):
        me = self.me
        return self.slot(((me.z + dz) % 4) * 4 + ((me.yh + fh) % 2) * 2 + (me.c + fc) % 2)

    def start(self):
        me, k, b, mine = self.me, self.k, self.b, self.at(0, 0)
        k.send(b + 1, self.own, mine, me.dev(fh=1))
        k.send(b + 2, self.own, mine, me.dev(dz=1))
        k.send(b + 3, self.own, mine, me.dev(dz=-1))
        k.send(b + 0, self.own, mine, me.dev(fc=1))

    def spread(self):
        me, k, b = self.me, self.k, self.b
        core = me.dev(fc=1)
        got = self.at(0, 1)
        k.arrived(b + 1, got, me.dev(fh=1))
        k.send(b + 4, got, got, me.dev(dz=1))
        k.send(b + 5, got, got, me.dev(dz=-1))
        k.send(b + 8, got, got, core)
        got = self.at(-1, 0)
        k.arrived(b + 2, got, me.dev(dz=-1))
        k.send(b + 6, got, got, me.dev(dz=1))
        k.send(b + 9, got, got, core)
        got = self.at(1, 0)
        k.arrived(b + 3, got, me.dev(dz=1))
        k.send(b + 11, got, got, core)
        got = self.at(1, 1)
        k.arrived(b + 5, got, me.dev(dz=1))
        k.send(b + 7, got, got, me.dev(dz=-1))
        k.send(b + 12, got, got, core)
        got = self.at(-1, 1)
        k.arrived(b + 4, got, me.dev(dz=-1))
        k.send(b + 10, got, got, core)

    def finish(self):
        me, k, b = self.me, self.k, self.b
        core = me.dev(fc=1)
        got = self.at(2, 0)
        k.arrived(b + 6, got, me.dev(dz=-1))
        k.send(b + 13, got, got, core)
        got = self.at(2, 1)
        k.arrived(b + 7, got, me.dev(dz=1))
        k.send(b + 14, got, got, core)
        for i, dz, fh in ((0, 0, 0), (8, 0, 1), (9, -1, 0), (10, -1, 1), (11, 1, 0), (12, 1, 1), (13, 2, 0), (14, 2, 1)):
            k.arrived(b + i, self.at(dz, fh, 1), core)


class RowGather:
    def __init__(self, me, copies, base, own, slots):
        self.me, self.k, self.b, self.own, self.slots = me, copies, base, own, slots
        self.half = own.shape[0] // 2

    def start(self):
        me, k, b = self.me, self.k, self.b
        k.send(b + 0, self.own, self.slots.at[me.x], me.dev(dx=1))
        k.send(b + 1, self.own, self.slots.at[me.x], me.dev(dx=-1))

    def spread(self):
        me, k, b, half = self.me, self.k, self.b, self.half
        left, right = (me.x + 3) % 4, (me.x + 1) % 4
        k.arrived(b + 0, self.slots.at[left], me.dev(dx=-1))
        part = self.slots.at[left, pl.ds(0, half)]
        k.send(b + 2, part, part, me.dev(dx=1))
        k.arrived(b + 1, self.slots.at[right], me.dev(dx=1))
        part = self.slots.at[right, pl.ds(half, half)]
        k.send(b + 3, part, part, me.dev(dx=-1))

    def finish(self):
        me, k, b, half = self.me, self.k, self.b, self.half
        far = (me.x + 2) % 4
        k.arrived(b + 2, self.slots.at[far, pl.ds(0, half)], me.dev(dx=-1))
        k.arrived(b + 3, self.slots.at[far, pl.ds(half, half)], me.dev(dx=1))


def gather_one(grad, acts, in_cut, grad_cut, all_grad, all_acts, in_x, grad_x, send, recv, local):
    me = Here()
    greet([me.dev(fc=1), me.dev(fh=1), me.dev(dz=1), me.dev(dz=-1), me.dev(dx=1), me.dev(dx=-1), me.dev(dx=2)])
    k = Copies(send, recv)
    rows = TensorGather(me, k, 0, grad, lambda t: all_grad.at[t])
    cols = RowGather(me, k, 15, acts, all_acts)
    rows.start()
    for i, dx in enumerate((1, 2, 3)):
        to = (me.x + dx) % 4
        k.send(19 + i, grad_cut.at[to], grad_x.at[me.x], me.dev(dx=dx))
        k.send(22 + i, in_cut.at[to], in_x.at[me.x], me.dev(dx=dx))
    cols.start()
    own = [
        pltpu.make_async_copy(grad, all_grad.at[me.t], local.at[0]),
        pltpu.make_async_copy(acts, all_acts.at[me.x], local.at[1]),
        pltpu.make_async_copy(grad_cut.at[me.x], grad_x.at[me.x], local.at[2]),
        pltpu.make_async_copy(in_cut.at[me.x], in_x.at[me.x], local.at[3]),
    ]
    for copy in own:
        copy.start()
    rows.spread()
    cols.spread()
    rows.finish()
    cols.finish()
    for i, dx in enumerate((1, 2, 3)):
        src = (me.x + 4 - dx) % 4
        k.arrived(19 + i, grad_x.at[src], me.dev(dx=-dx))
        k.arrived(22 + i, in_x.at[src], me.dev(dx=-dx))
    k.drain()
    for copy in own:
        copy.wait()


def gather_two(pre, in_x, grad_x, all_pre, in_all, grad_all, send, recv, local):
    me = Here()
    greet([me.dev(fc=1), me.dev(fh=1), me.dev(dz=1), me.dev(dz=-1), me.dev(dx=1), me.dev(dx=-1)])
    k = Copies(send, recv)
    one = TensorGather(me, k, 0, grad_x, lambda t: grad_all.at[:, t])
    two = TensorGather(me, k, 15, in_x, lambda t: in_all.at[:, t])
    cols = RowGather(me, k, 30, pre, all_pre)
    cols.start()
    one.start()
    two.start()
    own = [
        pltpu.make_async_copy(pre, all_pre.at[me.x], local.at[0]),
        pltpu.make_async_copy(grad_x, grad_all.at[:, me.t], local.at[1]),
        pltpu.make_async_copy(in_x, in_all.at[:, me.t], local.at[2]),
    ]
    for copy in own:
        copy.start()
    one.spread()
    cols.spread()
    two.spread()
    one.finish()
    two.finish()
    cols.finish()
    k.drain()
    for copy in own:
        copy.wait()


def blocks_at(blocks, table, rows, cols, width):
    return jnp.concatenate(
        [jnp.concatenate([blocks[table[r * width + j]] for j in cols], axis=1) for r in rows], axis=0
    )


def load_blocks(blocks, held, sem):
    copy = pltpu.make_async_copy(blocks, held.at[pl.ds(0, blocks.shape[0])], sem)
    copy.start()
    held[blocks.shape[0]] = jnp.zeros(held.shape[1:], held.dtype)
    copy.wait()


NT = (((1,), (1,)), ((), ()))
TN = (((0,), (0,)), ((), ()))


def pre_kernel(table, grad, blocks, hidden, out, held, acc, sem):
    k = pl.program_id(0)

    @pl.when(k == 0)
    def _():
        load_blocks(blocks, held, sem)

    acc[...] = jnp.zeros_like(acc)

    def step(i, _):
        j = i * 8
        w = blocks_at(held, table, (2 * k, 2 * k + 1), [j + a for a in range(8)], 96)
        left = grad[:, pl.ds(pl.multiple_of(j * 128, 1024), 1024)]
        acc[...] += lax.dot_general(left, w, NT, preferred_element_type=F32)
        return 0

    lax.fori_loop(0, 12, step, 0)
    out[...] = (acc[...] * gelu_slope(hidden[...].astype(F32))).astype(BF)


def back_kernel(table, pre, blocks, out, held, sem):
    i = pl.program_id(0)

    @pl.when(i == 0)
    def _():
        load_blocks(blocks, held, sem)

    def step(q, _):
        j = i * 8 + q * 2
        w = blocks_at(held, table, (j, j + 1), list(range(12)), 12)
        part = lax.dot_general(pre[...], w, NT, preferred_element_type=F32).astype(BF)
        for r in range(16):
            out[r % 2, r // 2, :, pl.ds(pl.multiple_of(q * 256, 256), 256)] = part[r * 16 : r * 16 + 16]
        return 0

    lax.fori_loop(0, 4, step, 0)


def grad_kernel(second, feat, hid, live, left, right, out, dense):
    i = pl.program_id(0)
    rows = left.shape[1]
    dense[pl.ds(pl.multiple_of(i * rows, rows), rows)] = lax.dot_general(
        left[...], right[...], TN, preferred_element_type=F32
    ).astype(BF)

    def tile(b):
        got = dense[pl.ds(pl.multiple_of(feat[b] * 32, 32), 32), pl.ds(pl.multiple_of(hid[b] * 128, 128), 128)]
        return jnp.where(b < live[0], got.astype(F32), 0.0)

    @pl.when(i == pl.num_programs(0) - 1)
    def _():
        def four(g, _):
            tiles = [tile(g * 4 + q) for q in range(4)]
            if second:
                turned = jnp.concatenate(tiles, axis=0).T.astype(BF)
                for s in range(8):
                    out[s % 2, s // 2, g] = turned[s * 16 : s * 16 + 16]
            else:
                for q in range(4):
                    got = tiles[q].astype(BF)
                    out[0, g * 4 + q] = got[:16]
                    out[1, g * 4 + q] = got[16:]
            return 0

        lax.fori_loop(0, 72, four, 0)


def scatter_kernel(
    part, one, two, out, first, second, own, mate, total, far_up, far_down, near_up, near_down, last, last_out,
    one_own, one_got, two_own, two_got, two_sum, two_all, send, recv, local,
):
    me = Here()
    greet([me.dev(fc=1), me.dev(fh=1), me.dev(dz=1), me.dev(dz=-1), me.dev(fl=1), me.dev(dx=1), me.dev(dx=-1), me.dev(dx=2)])
    k = Copies(send, recv)
    core, across, side = me.dev(fc=1), me.dev(fh=1), me.dev(fl=1)
    k.send(0, part.at[(me.c + 1) % 2], mate, core)
    k.send(1, two.at[(me.yl + 1) % 2], two_got, side)
    k.send(2, one.at[(me.yl + 1) % 2], one_got, side)
    mine = [
        pltpu.make_async_copy(part.at[me.c], own, local.at[0]),
        pltpu.make_async_copy(two.at[me.yl], two_own, local.at[1]),
        pltpu.make_async_copy(one.at[me.yl], one_own, local.at[2]),
    ]
    for copy in mine:
        copy.start()
    mine[0].wait()
    k.arrived(0, mate, core)

    def add_pair(i, _):
        total[i] = (own[i].astype(F32) + mate[i].astype(F32)).astype(BF)
        return 0

    z2, zu, zd = (me.z + 2) % 4, (me.z + 1) % 4, (me.z + 3) % 4
    lax.fori_loop(z2 * 2, z2 * 2 + 2, add_pair, 0)
    k.send(3, total.at[z2 * 2], far_up, me.dev(dz=1))
    k.send(4, total.at[z2 * 2 + 1], far_down, me.dev(dz=-1))
    lax.fori_loop(zu * 2, zu * 2 + 2, add_pair, 0)
    lax.fori_loop(zd * 2, zd * 2 + 2, add_pair, 0)
    lax.fori_loop(me.z * 2, me.z * 2 + 2, add_pair, 0)
    k.arrived(3, far_up, me.dev(dz=-1))
    total[zu * 2] = (total[zu * 2].astype(F32) + far_up[...].astype(F32)).astype(BF)
    k.send(5, total.at[pl.ds(zu * 2, 2)], near_up, me.dev(dz=1))
    k.arrived(4, far_down, me.dev(dz=1))
    total[zd * 2 + 1] = (total[zd * 2 + 1].astype(F32) + far_down[...].astype(F32)).astype(BF)
    k.send(6, total.at[pl.ds(zd * 2, 2)], near_down, me.dev(dz=-1))

    mine[1].wait()
    k.arrived(1, two_got, side)
    for dx in (2, 1, 3, 0):
        to = (me.x + dx) % 4

        def add_two(g, _):
            two_sum[to, g] = (two_own[to, g].astype(F32) + two_got[to, g].astype(F32)).astype(BF)
            return 0

        lax.fori_loop(0, 72, add_two, 0)
        if dx:
            k.send(6 + dx, two_sum.at[to], two_all.at[me.x], me.dev(dx=dx))
        else:
            two_all[me.x] = two_sum[me.x]

    k.arrived(5, near_up, me.dev(dz=-1))
    k.arrived(6, near_down, me.dev(dz=1))

    def add_three(h):
        return total[me.z * 2 + h].astype(F32) + near_up[h].astype(F32) + near_down[h].astype(F32)

    other = (me.yh + 1) % 2
    last_out[...] = add_three(other).astype(BF)
    k.send(10, last_out, last, across)
    mine[2].wait()
    k.arrived(2, one_got, side)

    def add_one(g, _):
        first[g] = (one_own[g].astype(F32) + one_got[g].astype(F32)).astype(BF)
        return 0

    lax.fori_loop(0, 288, add_one, 0)
    for dx in (1, 2, 3):
        k.arrived(6 + dx, two_all.at[(me.x + 4 - dx) % 4], me.dev(dx=-dx))

    def turn(g, _):
        for q in range(4):
            second[g * 4 + q] = jnp.concatenate([two_all[a, g][:, q * 32 : q * 32 + 32] for a in range(4)], axis=1)
        return 0

    lax.fori_loop(0, 72, turn, 0)
    k.arrived(10, last, across)
    out[...] = (add_three(me.yh) + last[...].astype(F32)).astype(BF)
    k.drain()


def sds(*shape):
    return jax.ShapeDtypeStruct(shape, BF)


def remote(kernel, number, outs, n_in, copies, locals_, scratch=(), specs=None, out_specs=None):
    return pl.pallas_call(
        kernel,
        out_shape=outs,
        in_specs=specs or [ANY] * n_in,
        out_specs=out_specs or tuple([ANY] * len(outs)),
        scratch_shapes=[
            *scratch,
            pltpu.SemaphoreType.DMA((copies,)),
            pltpu.SemaphoreType.DMA((copies,)),
            pltpu.SemaphoreType.DMA((locals_,)),
        ],
        compiler_params=pltpu.CompilerParams(
            collective_id=number, has_side_effects=True, vmem_limit_bytes=56 * MIB
        ),
    )


def shards(inputs, out_grad, hidden_pre, first_blocks, first_feat, first_hid, first_live, second_blocks, second_feat, second_hid, second_live):
    base = lax.axis_index("tensor") * 12
    hid_one, hid_two = first_hid - base, second_hid - base
    slots = jnp.arange(288, dtype=jnp.int32)
    cells = jnp.arange(1152, dtype=jnp.int32)
    cell_one = jnp.where(slots < first_live[0], first_feat * 12 + hid_one, -1)
    cell_two = jnp.where(slots < second_live[0], hid_two * 96 + second_feat, -1)
    table_one = jnp.min(jnp.where(cells[:, None] == cell_one[None], slots[None], 288), axis=1)
    table_two = jnp.min(jnp.where(cells[:, None] == cell_two[None], slots[None], 288), axis=1)
    acts = gelu_value(hidden_pre.astype(F32)).astype(BF)

    def cut(a):
        return a.reshape(16, 96, 4, 32).transpose(2, 0, 1, 3).reshape(4, 16, 3072)

    all_grad, all_acts, in_x, grad_x = remote(
        gather_one, 1, (sds(16, 16, 12288), sds(4, 256, 1536), sds(4, 16, 3072), sds(4, 16, 3072)), 4, 25, 4
    )(out_grad, acts, cut(inputs), cut(out_grad))

    pre = pl.pallas_call(
        pre_kernel,
        out_shape=sds(256, 1536),
        grid=(6,),
        in_specs=[SMEM, VMEM, ANY, pl.BlockSpec((256, 256), lambda k: (0, k))],
        out_specs=pl.BlockSpec((256, 256), lambda k: (0, k)),
        scratch_shapes=[pltpu.VMEM((289, 128, 128), BF), pltpu.VMEM((256, 256), F32), pltpu.SemaphoreType.DMA],
        compiler_params=pltpu.CompilerParams(vmem_limit_bytes=56 * MIB),
    )(table_two, all_grad.reshape(256, 12288), second_blocks, hidden_pre)

    all_pre, in_all, grad_all = remote(
        gather_two, 2, (sds(4, 256, 1536), sds(4, 16, 16, 3072), sds(4, 16, 16, 3072)), 3, 34, 3
    )(pre, in_x, grad_x)

    part = pl.pallas_call(
        back_kernel,
        out_shape=sds(2, 8, 16, 12288),
        grid=(12,),
        in_specs=[SMEM, VMEM, ANY],
        out_specs=pl.BlockSpec((2, 8, 16, 1024), lambda i: (0, 0, 0, i)),
        scratch_shapes=[pltpu.VMEM((289, 128, 128), BF), pltpu.SemaphoreType.DMA],
        compiler_params=pltpu.CompilerParams(vmem_limit_bytes=56 * MIB),
    )(table_one, pre, first_blocks)

    def block_grads(second, feat, hid, live, left, right):
        shape = (2, 4, 72, 16, 128) if second else (2, 288, 16, 128)
        return pl.pallas_call(
            functools.partial(grad_kernel, second),
            out_shape=sds(*shape),
            grid=(6,),
            in_specs=[SMEM, SMEM, SMEM, pl.BlockSpec((1024, 512), lambda i: (0, i)), VMEM],
            out_specs=pl.BlockSpec(shape, lambda i: (0,) * len(shape)),
            scratch_shapes=[pltpu.VMEM((3072, 1536), BF)],
            compiler_params=pltpu.CompilerParams(vmem_limit_bytes=56 * MIB),
        )(feat, hid, live, left.reshape(1024, 3072), right.reshape(1024, 1536))

    two = block_grads(True, second_feat, hid_two, second_live, grad_all, all_acts)
    one = block_grads(False, first_feat, hid_one, first_live, in_all, all_pre)

    pair = (2, 16, 12288)
    return remote(
        scatter_kernel,
        3,
        (sds(16, 12288), sds(288, 16, 128), sds(288, 16, 128)),
        3,
        11,
        3,
        scratch=[
            pltpu.VMEM((8, 16, 12288), BF),
            pltpu.VMEM((8, 16, 12288), BF),
            pltpu.VMEM((8, 16, 12288), BF),
            pltpu.VMEM((16, 12288), BF),
            pltpu.VMEM((16, 12288), BF),
            pltpu.VMEM(pair, BF),
            pltpu.VMEM(pair, BF),
            pltpu.VMEM((16, 12288), BF),
            pltpu.VMEM((16, 12288), BF),
            pltpu.VMEM((288, 16, 128), BF),
            pltpu.VMEM((288, 16, 128), BF),
            pltpu.VMEM((4, 72, 16, 128), BF),
            pltpu.VMEM((4, 72, 16, 128), BF),
            pltpu.VMEM((4, 72, 16, 128), BF),
            pltpu.VMEM((4, 72, 16, 128), BF),
        ],
        out_specs=(VMEM, VMEM, VMEM),
    )(part, one, two)


def solution(mesh):
    rows = P(("seq", "tensor"), None)
    cube = P("tensor", None, None)
    flat = P("tensor")
    in_specs = (rows, rows, P("seq", "tensor"), cube, flat, flat, flat, cube, flat, flat, flat)
    out_specs = (rows, P("tensor", "seq", None), P("tensor", "seq", None))
    return jax.shard_map(shards, mesh=mesh, in_specs=in_specs, out_specs=out_specs, check_vma=False)
```

```python
import jax
import jax.numpy as jnp
from jax import lax
from jax.experimental import pallas as pl
from jax.experimental.pallas import tpu as pltpu
from jax.sharding import PartitionSpec as P

MESH = pl.DeviceIdType.MESH
BF = jnp.bfloat16
F32 = jnp.float32
ANY = pl.BlockSpec(memory_space=pl.ANY)
SMEM = pl.BlockSpec(memory_space=pltpu.SMEM)
VMEM = pl.BlockSpec(memory_space=pltpu.VMEM)
MIB = 1024 * 1024

slope_coef = 0.7978845608028654
cubic_coef = 0.044715


def gelu_value(p):
    th = jnp.tanh(slope_coef * (p + cubic_coef * p * p * p))
    return 0.5 * p * (1.0 + th)


def gelu_slope(p):
    th = jnp.tanh(slope_coef * (p + cubic_coef * p * p * p))
    return 0.5 * (1.0 + th) + 0.5 * p * (1.0 - th * th) * slope_coef * (1.0 + 3.0 * cubic_coef * p * p)


class Here:
    def __init__(self):
        s = lax.axis_index("seq")
        t = lax.axis_index("tensor")
        self.s, self.t = s, t
        self.x, self.yl = s // 2, s % 2
        self.z, self.yh, self.c = t // 4, (t // 2) % 2, t % 2

    def dev(self, dx=0, fl=0, dz=0, fh=0, fc=0):
        x = (self.x + dx) % 4
        z = (self.z + dz) % 4
        yl = (self.yl + fl) % 2
        yh = (self.yh + fh) % 2
        c = (self.c + fc) % 2
        return (x * 2 + yl, z * 4 + yh * 2 + c)


class Copies:
    def __init__(self, send, recv):
        self.send_sems, self.recv_sems = send, recv
        self.sent = []

    def send(self, i, src, dst, device):
        copy = pltpu.make_async_remote_copy(
            src_ref=src,
            dst_ref=dst,
            send_sem=self.send_sems.at[i],
            recv_sem=self.recv_sems.at[i],
            device_id=device,
            device_id_type=MESH,
        )
        copy.start()
        self.sent.append(copy)

    def arrived(self, i, dst, device):
        pltpu.make_async_remote_copy(
            src_ref=dst,
            dst_ref=dst,
            send_sem=self.send_sems.at[i],
            recv_sem=self.recv_sems.at[i],
            device_id=device,
            device_id_type=MESH,
        ).wait_recv()

    def drain(self, count=None):
        for copy in self.sent[:count]:
            copy.wait_send()
        self.sent = self.sent[len(self.sent[:count]) :]


def greet(devices):
    barrier = pltpu.get_barrier_semaphore()
    for device in devices:
        pl.semaphore_signal(barrier, inc=1, device_id=device, device_id_type=MESH)
    pl.semaphore_wait(barrier, len(devices))


class TensorGather:
    def __init__(self, me, copies, base, own, slot):
        self.me, self.k, self.b, self.own, self.slot = me, copies, base, own, slot

    def at(self, dz, fh, fc=0):
        me = self.me
        return self.slot(((me.z + dz) % 4) * 4 + ((me.yh + fh) % 2) * 2 + (me.c + fc) % 2)

    def start(self):
        me, k, b, mine = self.me, self.k, self.b, self.at(0, 0)
        k.send(b + 1, self.own, mine, me.dev(fh=1))
        k.send(b + 2, self.own, mine, me.dev(dz=1))
        k.send(b + 3, self.own, mine, me.dev(dz=-1))
        k.send(b + 0, self.own, mine, me.dev(fc=1))

    def spread(self):
        me, k, b = self.me, self.k, self.b
        core = me.dev(fc=1)
        got = self.at(0, 1)
        k.arrived(b + 1, got, me.dev(fh=1))
        k.send(b + 4, got, got, me.dev(dz=1))
        k.send(b + 5, got, got, me.dev(dz=-1))
        k.send(b + 8, got, got, core)
        got = self.at(-1, 0)
        k.arrived(b + 2, got, me.dev(dz=-1))
        k.send(b + 6, got, got, me.dev(dz=1))
        k.send(b + 9, got, got, core)
        got = self.at(1, 0)
        k.arrived(b + 3, got, me.dev(dz=1))
        k.send(b + 11, got, got, core)
        got = self.at(1, 1)
        k.arrived(b + 5, got, me.dev(dz=1))
        k.send(b + 7, got, got, me.dev(dz=-1))
        k.send(b + 12, got, got, core)
        got = self.at(-1, 1)
        k.arrived(b + 4, got, me.dev(dz=-1))
        k.send(b + 10, got, got, core)

    def finish(self):
        me, k, b = self.me, self.k, self.b
        core = me.dev(fc=1)
        got = self.at(2, 0)
        k.arrived(b + 6, got, me.dev(dz=-1))
        k.send(b + 13, got, got, core)
        got = self.at(2, 1)
        k.arrived(b + 7, got, me.dev(dz=1))
        k.send(b + 14, got, got, core)
        for i, dz, fh in ((0, 0, 0), (8, 0, 1), (9, -1, 0), (10, -1, 1), (11, 1, 0), (12, 1, 1), (13, 2, 0), (14, 2, 1)):
            k.arrived(b + i, self.at(dz, fh, 1), core)


class RowGather:
    def __init__(self, me, copies, base, own, slots):
        self.me, self.k, self.b, self.own, self.slots = me, copies, base, own, slots
        self.half = own.shape[0] // 2

    def start(self):
        me, k, b = self.me, self.k, self.b
        k.send(b + 0, self.own, self.slots.at[me.x], me.dev(dx=1))
        k.send(b + 1, self.own, self.slots.at[me.x], me.dev(dx=-1))

    def spread(self):
        me, k, b, half = self.me, self.k, self.b, self.half
        left, right = (me.x + 3) % 4, (me.x + 1) % 4
        k.arrived(b + 0, self.slots.at[left], me.dev(dx=-1))
        part = self.slots.at[left, pl.ds(0, half)]
        k.send(b + 2, part, part, me.dev(dx=1))
        k.arrived(b + 1, self.slots.at[right], me.dev(dx=1))
        part = self.slots.at[right, pl.ds(half, half)]
        k.send(b + 3, part, part, me.dev(dx=-1))

    def finish(self):
        me, k, b, half = self.me, self.k, self.b, self.half
        far = (me.x + 2) % 4
        k.arrived(b + 2, self.slots.at[far, pl.ds(0, half)], me.dev(dx=-1))
        k.arrived(b + 3, self.slots.at[far, pl.ds(half, half)], me.dev(dx=1))


def blocks_at(blocks, table, rows, cols, width):
    return jnp.concatenate(
        [jnp.concatenate([blocks[table[r * width + j]] for j in cols], axis=1) for r in rows], axis=0
    )


NT = (((1,), (1,)), ((), ()))
TN = (((0,), (0,)), ((), ()))


def backward(
    table_one, table_two, tile_one, tile_two, inputs, grad, hidden, blocks_one, blocks_two,
    out, first, second, in_all, grad_all,
    rows, held, all_pre, all_acts, acc, in_cut, grad_cut, in_x, grad_x, mate, far_up, far_down, near_up, near_down, last,
    last_out, dense, lefts, one, one_got, two, two_got, two_sum, two_all, send, recv, local, chunk_sems,
):
    me = Here()
    greet([me.dev(fc=1), me.dev(fh=1), me.dev(dz=1), me.dev(dz=-1), me.dev(fl=1), me.dev(dx=1), me.dev(dx=-1), me.dev(dx=2)])
    k = Copies(send, recv)
    core, across, side = me.dev(fc=1), me.dev(fh=1), me.dev(fl=1)
    whole = TensorGather(me, k, 0, grad, lambda t: rows.at[t])
    grads = TensorGather(me, k, 15, grad_x, lambda t: grad_all.at[:, t])
    ins = TensorGather(me, k, 30, in_x, lambda t: in_all.at[:, t])
    pre_cols = RowGather(me, k, 45, all_pre.at[me.x], all_pre)
    act_cols = RowGather(me, k, 49, all_acts.at[me.x], all_acts)
    whole.start()
    rows[me.t] = grad[...]
    loads = [
        pltpu.make_async_copy(blocks, held.at[pl.ds(0, blocks.shape[0])], local.at[i])
        for i, blocks in enumerate((blocks_two, blocks_one))
    ]
    loads[0].start()
    held[blocks_two.shape[0]] = jnp.zeros(held.shape[1:], held.dtype)
    dense[dense.shape[0] - 1] = jnp.zeros(dense.shape[1:], dense.dtype)

    def cut(source, parts):
        def step(g, _):
            wide = source[:, pl.ds(pl.multiple_of(g * 512, 512), 512)].astype(F32)
            for a in range(4):
                got = jnp.concatenate([wide[:, q * 128 + a * 32 : q * 128 + a * 32 + 32] for q in range(4)], axis=1)
                parts[a, :, pl.ds(pl.multiple_of(g * 128, 128), 128)] = got.astype(BF)
            return 0

        lax.fori_loop(0, 24, step, 0)

    cut(grad, grad_cut)
    for dx in (1, 2, 3):
        k.send(52 + dx, grad_cut.at[(me.x + dx) % 4], grad_x.at[me.x], me.dev(dx=dx))
    cut(inputs, in_cut)
    for dx in (1, 2, 3):
        k.send(55 + dx, in_cut.at[(me.x + dx) % 4], in_x.at[me.x], me.dev(dx=dx))
    grad_x[me.x] = grad_cut[me.x]
    in_x[me.x] = in_cut[me.x]

    def act(i, _):
        span = pl.ds(pl.multiple_of(i * 16, 16), 16)
        all_acts[me.x, span] = gelu_value(hidden[span].astype(F32)).astype(BF)
        return 0

    lax.fori_loop(0, 16, act, 0)
    act_cols.start()
    whole.spread()
    for dx in (1, 2, 3):
        k.arrived(52 + dx, grad_x.at[(me.x + 4 - dx) % 4], me.dev(dx=-dx))
    grads.start()
    mine = [
        pltpu.make_async_copy(grad_x, grad_all.at[:, me.t], local.at[2]),
        pltpu.make_async_copy(in_x, in_all.at[:, me.t], local.at[3]),
    ]
    mine[0].start()
    act_cols.spread()
    for dx in (1, 2, 3):
        k.arrived(55 + dx, in_x.at[(me.x + 4 - dx) % 4], me.dev(dx=-dx))
    mine[1].start()
    whole.finish()
    settled = len(k.sent)
    ins.start()
    loads[0].wait()

    def pre(n, _):
        acc[...] = jnp.zeros_like(acc)

        def step(i, _):
            j = i * 16
            w = blocks_at(held, table_two, (2 * n, 2 * n + 1), [j + a for a in range(16)], 96)
            left = rows[:, :, pl.ds(pl.multiple_of(j * 128, 2048), 2048)].reshape(256, 2048)
            acc[...] += lax.dot_general(left, w, NT, preferred_element_type=F32)
            return 0

        lax.fori_loop(0, 6, step, 0)
        span = pl.ds(pl.multiple_of(n * 256, 256), 256)
        all_pre[me.x, :, span] = (acc[...] * gelu_slope(hidden[:, span].astype(F32))).astype(BF)
        return 0

    lax.fori_loop(0, 2, pre, 0)
    grads.spread()
    lax.fori_loop(2, 4, pre, 0)
    ins.spread()
    lax.fori_loop(4, 6, pre, 0)
    pre_cols.start()
    loads[1].start()

    def block_products(source, right):
        def fetch(i):
            return pltpu.make_async_copy(
                source.at[:, :, :, pl.ds(pl.multiple_of(i * 512, 512), 512)], lefts.at[i % 2], chunk_sems.at[i % 2]
            )

        fetch(0).start()

        def step(i, _):
            @pl.when(i < 5)
            def _():
                fetch(i + 1).start()

            fetch(i).wait()
            got = lax.dot_general(
                lefts[i % 2].reshape(1024, 512), right[...].reshape(1024, 1536), TN, preferred_element_type=F32
            ).astype(BF)
            for a in range(16):
                for h in range(12):
                    dense[(i * 16 + a) * 12 + h] = got[a * 32 : a * 32 + 32, h * 128 : h * 128 + 128]
            return 0

        lax.fori_loop(0, 6, step, 0)

    grads.finish()
    act_cols.finish()
    mine[0].wait()
    block_products(grad_all, all_acts)

    def cut_two(g, _):
        tiles = [dense[tile_two[g * 4 + q]].astype(F32) for q in range(4)]
        turned = jnp.concatenate(tiles, axis=0).T.astype(BF)
        for s in range(8):
            two[s % 2, s // 2, g] = turned[s * 16 : s * 16 + 16]
        return 0

    lax.fori_loop(0, 72, cut_two, 0)
    k.send(65, two.at[(me.yl + 1) % 2], two_got, side)
    pre_cols.spread()
    loads[1].wait()
    k.drain(settled)

    def back(q):
        def step(i, _):
            j = q * 24 + i * 4
            w = blocks_at(held, table_one, [j + a for a in range(4)], list(range(12)), 12)
            got = lax.dot_general(all_pre[me.x], w, NT, preferred_element_type=F32).astype(BF)
            for r in range(16):
                rows[r % 2 * 8 + r // 2, :, pl.ds(pl.multiple_of(j * 128, 512), 512)] = got[r * 16 : r * 16 + 16]
            return 0

        lax.fori_loop(0, 6, step, 0)
        span = pl.ds(q * 3072, 3072)
        k.send(59 + q, rows.at[pl.ds((me.c + 1) % 2 * 8, 8), :, span], mate.at[:, :, span], core)

    back(0)
    back(1)
    ins.finish()
    back(2)
    back(3)
    own = rows.at[pl.ds(me.c * 8, 8)]

    def add_pair(i, _):
        own[i] = (own[i].astype(F32) + mate[i].astype(F32)).astype(BF)
        return 0

    for q in range(4):
        k.arrived(59 + q, mate.at[:, :, pl.ds(q * 3072, 3072)], core)
    z2, zu, zd = (me.z + 2) % 4, (me.z + 1) % 4, (me.z + 3) % 4
    lax.fori_loop(z2 * 2, z2 * 2 + 2, add_pair, 0)
    k.send(63, own.at[z2 * 2], far_up, me.dev(dz=1))
    k.send(64, own.at[z2 * 2 + 1], far_down, me.dev(dz=-1))
    lax.fori_loop(zu * 2, zu * 2 + 2, add_pair, 0)
    lax.fori_loop(zd * 2, zd * 2 + 2, add_pair, 0)
    lax.fori_loop(me.z * 2, me.z * 2 + 2, add_pair, 0)

    k.arrived(63, far_up, me.dev(dz=-1))
    own[zu * 2] = (own[zu * 2].astype(F32) + far_up[...].astype(F32)).astype(BF)
    k.send(66, own.at[pl.ds(zu * 2, 2)], near_up, me.dev(dz=1))
    k.arrived(64, far_down, me.dev(dz=1))
    own[zd * 2 + 1] = (own[zd * 2 + 1].astype(F32) + far_down[...].astype(F32)).astype(BF)
    k.send(67, own.at[pl.ds(zd * 2, 2)], near_down, me.dev(dz=-1))

    pre_cols.finish()
    mine[1].wait()
    block_products(in_all, all_pre)

    def cut_one(g, _):
        for q in range(4):
            b = g * 4 + q
            got = dense[tile_one[b]]
            one[0, b] = got[:16]
            one[1, b] = got[16:]
        return 0

    lax.fori_loop(0, 72, cut_one, 0)
    k.send(68, one.at[(me.yl + 1) % 2], one_got, side)

    k.arrived(66, near_up, me.dev(dz=-1))
    k.arrived(67, near_down, me.dev(dz=1))

    def add_three(h):
        return own[me.z * 2 + h].astype(F32) + near_up[h].astype(F32) + near_down[h].astype(F32)

    last_out[...] = add_three((me.yh + 1) % 2).astype(BF)
    k.send(69, last_out, last, across)

    k.arrived(65, two_got, side)
    for dx in (2, 1, 3, 0):
        to = (me.x + dx) % 4

        def add_two(g, _):
            two_sum[to, g] = (two[me.yl, to, g].astype(F32) + two_got[to, g].astype(F32)).astype(BF)
            return 0

        lax.fori_loop(0, 72, add_two, 0)
        if dx:
            k.send(69 + dx, two_sum.at[to], two_all.at[me.x], me.dev(dx=dx))
        else:
            two_all[me.x] = two_sum[me.x]

    k.arrived(69, last, across)
    out[...] = (add_three(me.yh) + last[...].astype(F32)).astype(BF)
    for dx in (1, 2, 3):
        k.arrived(69 + dx, two_all.at[(me.x + 4 - dx) % 4], me.dev(dx=-dx))

    def turn(g, _):
        for q in range(4):
            second[g * 4 + q] = jnp.concatenate([two_all[a, g][:, q * 32 : q * 32 + 32] for a in range(4)], axis=1)
        return 0

    lax.fori_loop(0, 72, turn, 0)
    k.arrived(68, one_got, side)

    def add_one(g, _):
        first[g] = (one[me.yl, g].astype(F32) + one_got[g].astype(F32)).astype(BF)
        return 0

    lax.fori_loop(0, 288, add_one, 0)
    k.drain()


def sds(*shape):
    return jax.ShapeDtypeStruct(shape, BF)


def shards(inputs, out_grad, hidden_pre, first_blocks, first_feat, first_hid, first_live, second_blocks, second_feat, second_hid, second_live):
    base = lax.axis_index("tensor") * 12
    hid_one, hid_two = first_hid - base, second_hid - base
    slots = jnp.arange(288, dtype=jnp.int32)
    cells = jnp.arange(1152, dtype=jnp.int32)
    cell_one = jnp.where(slots < first_live[0], first_feat * 12 + hid_one, -1)
    cell_two = jnp.where(slots < second_live[0], hid_two * 96 + second_feat, -1)
    table_one = jnp.min(jnp.where(cells[:, None] == cell_one[None], slots[None], 288), axis=1)
    table_two = jnp.min(jnp.where(cells[:, None] == cell_two[None], slots[None], 288), axis=1)
    tile_one = jnp.where(slots < first_live[0], first_feat * 12 + hid_one, 1152)
    tile_two = jnp.where(slots < second_live[0], second_feat * 12 + hid_two, 1152)
    row, pair, half, quarter = (16, 12288), (2, 16, 12288), (8, 16, 12288), (4, 16, 3072)
    shapes = [
        (16, 16, 12288), (289, 128, 128), (4, 256, 1536), (4, 256, 1536), None, quarter, quarter, quarter, quarter, half, row, row,
        pair, pair, row, row, (1153, 32, 128), (2, 4, 16, 16, 512), (2, 288, 16, 128), (288, 16, 128), (2, 4, 72, 16, 128),
        (4, 72, 16, 128), (4, 72, 16, 128), (4, 72, 16, 128),
    ]
    return pl.pallas_call(
        backward,
        out_shape=(sds(*row), sds(288, 16, 128), sds(288, 16, 128), sds(4, 16, 16, 3072), sds(4, 16, 16, 3072)),
        in_specs=[SMEM] * 4 + [VMEM] * 3 + [ANY] * 2,
        out_specs=(VMEM, VMEM, VMEM, ANY, ANY),
        scratch_shapes=[
            *[pltpu.VMEM(shape, BF) if shape else pltpu.VMEM((256, 256), F32) for shape in shapes],
            pltpu.SemaphoreType.DMA((73,)),
            pltpu.SemaphoreType.DMA((73,)),
            pltpu.SemaphoreType.DMA((4,)),
            pltpu.SemaphoreType.DMA((2,)),
        ],
        compiler_params=pltpu.CompilerParams(collective_id=1, has_side_effects=True, vmem_limit_bytes=60 * MIB),
    )(table_one, table_two, tile_one, tile_two, inputs, out_grad, hidden_pre, first_blocks, second_blocks)[:3]


def solution(mesh):
    rows = P(("seq", "tensor"), None)
    cube = P("tensor", None, None)
    flat = P("tensor")
    in_specs = (rows, rows, P("seq", "tensor"), cube, flat, flat, flat, cube, flat, flat, flat)
    out_specs = (rows, P("tensor", "seq", None), P("tensor", "seq", None))
    return jax.shard_map(shards, mesh=mesh, in_specs=in_specs, out_specs=out_specs, check_vma=False)
```

```python
import jax
import jax.numpy as jnp
from jax import lax
from jax.experimental import pallas as pl
from jax.experimental.pallas import tpu as pltpu
from jax.sharding import PartitionSpec as P

MESH = pl.DeviceIdType.MESH
BF = jnp.bfloat16
F32 = jnp.float32
ANY = pl.BlockSpec(memory_space=pl.ANY)
SMEM = pl.BlockSpec(memory_space=pltpu.SMEM)
VMEM = pl.BlockSpec(memory_space=pltpu.VMEM)
MIB = 1024 * 1024

slope_coef = 0.7978845608028654
cubic_coef = 0.044715


def gelu_value(p):
    th = jnp.tanh(slope_coef * (p + cubic_coef * p * p * p))
    return 0.5 * p * (1.0 + th)


def gelu_slope(p):
    th = jnp.tanh(slope_coef * (p + cubic_coef * p * p * p))
    return 0.5 * (1.0 + th) + 0.5 * p * (1.0 - th * th) * slope_coef * (1.0 + 3.0 * cubic_coef * p * p)


class Here:
    def __init__(self):
        s = lax.axis_index("seq")
        t = lax.axis_index("tensor")
        self.s, self.t = s, t
        self.x, self.yl = s // 2, s % 2
        self.z, self.yh, self.c = t // 4, (t // 2) % 2, t % 2

    def dev(self, dx=0, fl=0, dz=0, fh=0, fc=0):
        x = (self.x + dx) % 4
        z = (self.z + dz) % 4
        yl = (self.yl + fl) % 2
        yh = (self.yh + fh) % 2
        c = (self.c + fc) % 2
        return (x * 2 + yl, z * 4 + yh * 2 + c)


class Copies:
    def __init__(self, send, recv):
        self.send_sems, self.recv_sems = send, recv
        self.sent = []

    def send(self, i, src, dst, device):
        copy = pltpu.make_async_remote_copy(
            src_ref=src,
            dst_ref=dst,
            send_sem=self.send_sems.at[i],
            recv_sem=self.recv_sems.at[i],
            device_id=device,
            device_id_type=MESH,
        )
        copy.start()
        self.sent.append(copy)

    def arrived(self, i, dst, device):
        pltpu.make_async_remote_copy(
            src_ref=dst,
            dst_ref=dst,
            send_sem=self.send_sems.at[i],
            recv_sem=self.recv_sems.at[i],
            device_id=device,
            device_id_type=MESH,
        ).wait_recv()

    def drain(self, count=None):
        for copy in self.sent[:count]:
            copy.wait_send()
        self.sent = self.sent[len(self.sent[:count]) :]


def greet(devices):
    barrier = pltpu.get_barrier_semaphore()
    for device in devices:
        pl.semaphore_signal(barrier, inc=1, device_id=device, device_id_type=MESH)
    pl.semaphore_wait(barrier, len(devices))


class TensorGather:
    def __init__(self, me, copies, base, own, slot):
        self.me, self.k, self.b, self.own, self.slot = me, copies, base, own, slot

    def at(self, dz, fh, fc=0):
        me = self.me
        return self.slot(((me.z + dz) % 4) * 4 + ((me.yh + fh) % 2) * 2 + (me.c + fc) % 2)

    def start(self):
        me, k, b, mine = self.me, self.k, self.b, self.at(0, 0)
        k.send(b + 1, self.own, mine, me.dev(fh=1))
        k.send(b + 2, self.own, mine, me.dev(dz=1))
        k.send(b + 3, self.own, mine, me.dev(dz=-1))
        k.send(b + 0, self.own, mine, me.dev(fc=1))

    def spread(self):
        me, k, b = self.me, self.k, self.b
        core = me.dev(fc=1)
        got = self.at(0, 1)
        k.arrived(b + 1, got, me.dev(fh=1))
        k.send(b + 4, got, got, me.dev(dz=1))
        k.send(b + 5, got, got, me.dev(dz=-1))
        k.send(b + 8, got, got, core)
        got = self.at(-1, 0)
        k.arrived(b + 2, got, me.dev(dz=-1))
        k.send(b + 6, got, got, me.dev(dz=1))
        k.send(b + 9, got, got, core)
        got = self.at(1, 0)
        k.arrived(b + 3, got, me.dev(dz=1))
        k.send(b + 11, got, got, core)
        got = self.at(1, 1)
        k.arrived(b + 5, got, me.dev(dz=1))
        k.send(b + 7, got, got, me.dev(dz=-1))
        k.send(b + 12, got, got, core)
        got = self.at(-1, 1)
        k.arrived(b + 4, got, me.dev(dz=-1))
        k.send(b + 10, got, got, core)

    def finish(self):
        me, k, b = self.me, self.k, self.b
        core = me.dev(fc=1)
        got = self.at(2, 0)
        k.arrived(b + 6, got, me.dev(dz=-1))
        k.send(b + 13, got, got, core)
        got = self.at(2, 1)
        k.arrived(b + 7, got, me.dev(dz=1))
        k.send(b + 14, got, got, core)
        for i, dz, fh in ((0, 0, 0), (8, 0, 1), (9, -1, 0), (10, -1, 1), (11, 1, 0), (12, 1, 1), (13, 2, 0), (14, 2, 1)):
            k.arrived(b + i, self.at(dz, fh, 1), core)


class RowGather:
    def __init__(self, me, copies, base, own, slots):
        self.me, self.k, self.b, self.own, self.slots = me, copies, base, own, slots
        self.half = own.shape[0] // 2

    def start(self):
        me, k, b = self.me, self.k, self.b
        k.send(b + 0, self.own, self.slots.at[me.x], me.dev(dx=1))
        k.send(b + 1, self.own, self.slots.at[me.x], me.dev(dx=-1))

    def spread(self):
        me, k, b, half = self.me, self.k, self.b, self.half
        left, right = (me.x + 3) % 4, (me.x + 1) % 4
        k.arrived(b + 0, self.slots.at[left], me.dev(dx=-1))
        part = self.slots.at[left, pl.ds(0, half)]
        k.send(b + 2, part, part, me.dev(dx=1))
        k.arrived(b + 1, self.slots.at[right], me.dev(dx=1))
        part = self.slots.at[right, pl.ds(half, half)]
        k.send(b + 3, part, part, me.dev(dx=-1))

    def finish(self):
        me, k, b, half = self.me, self.k, self.b, self.half
        far = (me.x + 2) % 4
        k.arrived(b + 2, self.slots.at[far, pl.ds(0, half)], me.dev(dx=-1))
        k.arrived(b + 3, self.slots.at[far, pl.ds(half, half)], me.dev(dx=1))


class SeqGather:
    def __init__(self, me, copies, base, slots):
        self.me, self.k, self.b, self.slots = me, copies, base, slots

    def at(self, dx, fl):
        me = self.me
        return self.slots.at[(me.x + dx) % 4 * 2 + (me.yl + fl) % 2]

    def half(self, dx, i):
        me = self.me
        return self.slots.at[(me.x + dx) % 4 * 2 + me.yl, pl.ds(i * 128, 128)]

    def start(self):
        me, k, b = self.me, self.k, self.b
        own = self.at(0, 0)
        k.send(b + 2, own, own, me.dev(fl=1))
        k.send(b + 0, own, own, me.dev(dx=1))
        k.send(b + 1, own, own, me.dev(dx=-1))

    def spread(self):
        me, k, b = self.me, self.k, self.b
        k.arrived(b + 0, self.at(-1, 0), me.dev(dx=-1))
        part = self.half(-1, 0)
        k.send(b + 3, part, part, me.dev(dx=1))
        k.arrived(b + 1, self.at(1, 0), me.dev(dx=1))
        part = self.half(1, 1)
        k.send(b + 4, part, part, me.dev(dx=-1))
        got = self.at(0, 1)
        k.arrived(b + 2, got, me.dev(fl=1))
        k.send(b + 5, got, got, me.dev(dx=1))
        k.send(b + 6, got, got, me.dev(dx=-1))

    def cross(self):
        me, k, b = self.me, self.k, self.b
        k.arrived(b + 3, self.half(2, 0), me.dev(dx=-1))
        k.arrived(b + 4, self.half(2, 1), me.dev(dx=1))
        got = self.at(2, 0)
        k.send(b + 7, got, got, me.dev(fl=1))

    def finish(self):
        me, k, b = self.me, self.k, self.b
        k.arrived(b + 5, self.at(-1, 1), me.dev(dx=-1))
        k.arrived(b + 6, self.at(1, 1), me.dev(dx=1))
        k.arrived(b + 7, self.at(2, 1), me.dev(fl=1))


def blocks_at(blocks, table, rows, cols, width):
    return jnp.concatenate(
        [jnp.concatenate([blocks[table[r * width + j]] for j in cols], axis=1) for r in rows], axis=0
    )


NT = (((1,), (1,)), ((), ()))
TN = (((0,), (0,)), ((), ()))


def backward(
    table_one, table_two, tile_one, tile_two, inputs, grad, hidden, blocks_one, blocks_two,
    out, first, second, in_all, grad_all,
    rows, held, all_pre, all_acts, acc, in_cut, grad_cut, in_x, grad_x, mate, far_up, far_down, near_up, near_down, last,
    last_out, dense, lefts, in_lefts, two, two_got, two_sum, two_all, send, recv, local, chunk_sems,
):
    me = Here()
    greet([me.dev(fc=1), me.dev(fh=1), me.dev(dz=1), me.dev(dz=-1), me.dev(fl=1), me.dev(dx=1), me.dev(dx=-1), me.dev(dx=2)] + [me.dev(dx=dx, fl=1) for dx in (1, 2, 3)])
    k = Copies(send, recv)
    core, across, side = me.dev(fc=1), me.dev(fh=1), me.dev(fl=1)
    whole = TensorGather(me, k, 0, grad, lambda t: rows.at[t])
    grads = TensorGather(me, k, 15, grad_x, lambda t: grad_all.at[:, t])
    ins = TensorGather(me, k, 30, in_x, lambda t: in_all.at[:, t])
    pre_cols = SeqGather(me, k, 45, all_pre)
    act_cols = RowGather(me, k, 53, all_acts.at[me.x], all_acts)
    whole.start()
    rows[me.t] = grad[...]
    loads = [
        pltpu.make_async_copy(blocks, held.at[pl.ds(0, blocks.shape[0])], local.at[i])
        for i, blocks in enumerate((blocks_two, blocks_one))
    ]
    loads[0].start()
    held[blocks_two.shape[0]] = jnp.zeros(held.shape[1:], held.dtype)
    dense[dense.shape[0] - 1] = jnp.zeros(dense.shape[1:], dense.dtype)

    def cut(source, parts, n):
        wide, thin = n * 128, 128 // n

        def step(g, _):
            got = source[:, pl.ds(pl.multiple_of(g * wide, wide), wide)].astype(F32)
            for a in range(n):
                part = jnp.concatenate([got[:, q * 128 + a * thin : q * 128 + a * thin + thin] for q in range(n)], axis=1)
                parts[a, :, pl.ds(pl.multiple_of(g * 128, 128), 128)] = part.astype(BF)
            return 0

        lax.fori_loop(0, 96 // n, step, 0)

    cut(grad, grad_cut, 4)
    for dx in (1, 2, 3):
        k.send(56 + dx, grad_cut.at[(me.x + dx) % 4], grad_x.at[me.x], me.dev(dx=dx))
    grad_x[me.x] = grad_cut[me.x]

    def act(i, _):
        span = pl.ds(pl.multiple_of(i * 16, 16), 16)
        all_acts[me.x, span] = gelu_value(hidden[span].astype(F32)).astype(BF)
        return 0

    lax.fori_loop(0, 16, act, 0)
    act_cols.start()
    whole.spread()
    for dx in (1, 2, 3):
        k.arrived(56 + dx, grad_x.at[(me.x + 4 - dx) % 4], me.dev(dx=-dx))
    grads.start()
    mine = [
        pltpu.make_async_copy(grad_x, grad_all.at[:, me.t], local.at[2]),
        pltpu.make_async_copy(in_x, in_all.at[:, me.t], local.at[3]),
    ]
    mine[0].start()
    cut(inputs, in_cut, 8)
    others = [(dx, fl) for dx in range(4) for fl in range(2)][1:]
    for i, (dx, fl) in enumerate(others):
        to = (me.x + dx) % 4 * 2 + (me.yl + fl) % 2
        k.send(60 + i, in_cut.at[to], in_x.at[me.s], me.dev(dx=dx, fl=fl))
    in_x[me.s] = in_cut[me.s]
    act_cols.spread()
    whole.finish()
    settled = len(k.sent)
    loads[0].wait()

    def pre(n, _):
        acc[...] = jnp.zeros_like(acc)

        def step(i, _):
            j = i * 16
            w = blocks_at(held, table_two, (2 * n, 2 * n + 1), [j + a for a in range(16)], 96)
            left = rows[:, :, pl.ds(pl.multiple_of(j * 128, 2048), 2048)].reshape(256, 2048)
            acc[...] += lax.dot_general(left, w, NT, preferred_element_type=F32)
            return 0

        lax.fori_loop(0, 6, step, 0)
        span = pl.ds(pl.multiple_of(n * 256, 256), 256)
        all_pre[me.s, :, span] = (acc[...] * gelu_slope(hidden[:, span].astype(F32))).astype(BF)
        return 0

    lax.fori_loop(0, 2, pre, 0)
    grads.spread()
    lax.fori_loop(2, 4, pre, 0)
    for i, (dx, fl) in enumerate(others):
        k.arrived(60 + i, in_x.at[(me.x + 4 - dx) % 4 * 2 + (me.yl + fl) % 2], me.dev(dx=-dx, fl=fl))
    mine[1].start()
    ins.start()
    lax.fori_loop(4, 6, pre, 0)
    pre_cols.start()
    loads[1].start()

    def block_products(source, buffers, right, cuts, first_step, last_step):
        tall, wide = cuts * 256, 2048 // cuts
        thin = wide // 16

        def fetch(i):
            return pltpu.make_async_copy(
                source.at[:, :, :, pl.ds(pl.multiple_of(i * wide, wide), wide)], buffers.at[i % 2], chunk_sems.at[i % 2]
            )

        if first_step == 0:
            fetch(0).start()

        def step(i, _):
            @pl.when(i < 5)
            def _():
                fetch(i + 1).start()

            fetch(i).wait()
            got = lax.dot_general(
                buffers[i % 2].reshape(tall, wide), right[...].reshape(tall, 1536), TN, preferred_element_type=F32
            ).astype(BF)
            for a in range(16):
                for h in range(12):
                    dense[(i * 16 + a) * 12 + h, :thin] = got[a * thin : a * thin + thin, h * 128 : h * 128 + 128]
            return 0

        lax.fori_loop(first_step, last_step, step, 0)

    grads.finish()
    act_cols.finish()
    mine[0].wait()
    block_products(grad_all, lefts, all_acts, 4, 0, 6)
    ins.spread()
    pre_cols.spread()

    def cut_two(g, _):
        tiles = [dense[tile_two[g * 4 + q]].astype(F32) for q in range(4)]
        turned = jnp.concatenate(tiles, axis=0).T.astype(BF)
        for s in range(8):
            two[s % 2, s // 2, g] = turned[s * 16 : s * 16 + 16]
        return 0

    lax.fori_loop(0, 72, cut_two, 0)
    k.send(73, two.at[(me.yl + 1) % 2], two_got, side)
    loads[1].wait()
    k.drain(settled)

    def back(q):
        def step(i, _):
            j = q * 24 + i * 4
            w = blocks_at(held, table_one, [j + a for a in range(4)], list(range(12)), 12)
            got = lax.dot_general(all_pre[me.s], w, NT, preferred_element_type=F32).astype(BF)
            for r in range(16):
                rows[r % 2 * 8 + r // 2, :, pl.ds(pl.multiple_of(j * 128, 512), 512)] = got[r * 16 : r * 16 + 16]
            return 0

        lax.fori_loop(0, 6, step, 0)
        span = pl.ds(q * 3072, 3072)
        k.send(67 + q, rows.at[pl.ds((me.c + 1) % 2 * 8, 8), :, span], mate.at[:, :, span], core)

    back(0)
    back(1)
    back(2)
    pre_cols.cross()
    back(3)
    ins.finish()
    own = rows.at[pl.ds(me.c * 8, 8)]

    def add_pair(i, _):
        own[i] = (own[i].astype(F32) + mate[i].astype(F32)).astype(BF)
        return 0

    for q in range(4):
        k.arrived(67 + q, mate.at[:, :, pl.ds(q * 3072, 3072)], core)
    z2, zu, zd = (me.z + 2) % 4, (me.z + 1) % 4, (me.z + 3) % 4
    lax.fori_loop(z2 * 2, z2 * 2 + 2, add_pair, 0)
    k.send(71, own.at[z2 * 2], far_up, me.dev(dz=1))
    k.send(72, own.at[z2 * 2 + 1], far_down, me.dev(dz=-1))
    lax.fori_loop(zu * 2, zu * 2 + 2, add_pair, 0)
    lax.fori_loop(zd * 2, zd * 2 + 2, add_pair, 0)
    lax.fori_loop(me.z * 2, me.z * 2 + 2, add_pair, 0)

    pre_cols.finish()
    mine[1].wait()
    block_products(in_all, in_lefts, all_pre, 8, 0, 3)

    k.arrived(71, far_up, me.dev(dz=-1))
    own[zu * 2] = (own[zu * 2].astype(F32) + far_up[...].astype(F32)).astype(BF)
    k.send(74, own.at[pl.ds(zu * 2, 2)], near_up, me.dev(dz=1))
    k.arrived(72, far_down, me.dev(dz=1))
    own[zd * 2 + 1] = (own[zd * 2 + 1].astype(F32) + far_down[...].astype(F32)).astype(BF)
    k.send(75, own.at[pl.ds(zd * 2, 2)], near_down, me.dev(dz=-1))

    k.arrived(73, two_got, side)
    for dx in (2, 1, 3, 0):
        to = (me.x + dx) % 4

        def add_two(g, _):
            two_sum[to, g] = (two[me.yl, to, g].astype(F32) + two_got[to, g].astype(F32)).astype(BF)
            return 0

        lax.fori_loop(0, 72, add_two, 0)
        if dx:
            k.send(76 + dx, two_sum.at[to], two_all.at[me.x], me.dev(dx=dx))
        else:
            two_all[me.x] = two_sum[me.x]

    block_products(in_all, in_lefts, all_pre, 8, 3, 6)

    k.arrived(74, near_up, me.dev(dz=-1))
    k.arrived(75, near_down, me.dev(dz=1))

    def add_three(h):
        return own[me.z * 2 + h].astype(F32) + near_up[h].astype(F32) + near_down[h].astype(F32)

    last_out[...] = add_three((me.yh + 1) % 2).astype(BF)
    k.send(76, last_out, last, across)

    def cut_one(g, _):
        for q in range(4):
            first[g * 4 + q] = dense[tile_one[g * 4 + q]][:16]
        return 0

    lax.fori_loop(0, 72, cut_one, 0)
    for dx in (1, 2, 3):
        k.arrived(76 + dx, two_all.at[(me.x + 4 - dx) % 4], me.dev(dx=-dx))

    def turn(g, _):
        for q in range(4):
            second[g * 4 + q] = jnp.concatenate([two_all[a, g][:, q * 32 : q * 32 + 32] for a in range(4)], axis=1)
        return 0

    lax.fori_loop(0, 72, turn, 0)
    k.arrived(76, last, across)
    out[...] = (add_three(me.yh) + last[...].astype(F32)).astype(BF)
    k.drain()


def sds(*shape):
    return jax.ShapeDtypeStruct(shape, BF)


def shards(inputs, out_grad, hidden_pre, first_blocks, first_feat, first_hid, first_live, second_blocks, second_feat, second_hid, second_live):
    base = lax.axis_index("tensor") * 12
    hid_one, hid_two = first_hid - base, second_hid - base
    slots = jnp.arange(288, dtype=jnp.int32)
    cells = jnp.arange(1152, dtype=jnp.int32)
    cell_one = jnp.where(slots < first_live[0], first_feat * 12 + hid_one, -1)
    cell_two = jnp.where(slots < second_live[0], hid_two * 96 + second_feat, -1)
    table_one = jnp.min(jnp.where(cells[:, None] == cell_one[None], slots[None], 288), axis=1)
    table_two = jnp.min(jnp.where(cells[:, None] == cell_two[None], slots[None], 288), axis=1)
    tile_one = jnp.where(slots < first_live[0], first_feat * 12 + hid_one, 1152)
    tile_two = jnp.where(slots < second_live[0], second_feat * 12 + hid_two, 1152)
    row, pair, half, quarter, eighth = (16, 12288), (2, 16, 12288), (8, 16, 12288), (4, 16, 3072), (8, 16, 1536)
    shapes = [
        (16, 16, 12288), (289, 128, 128), (8, 256, 1536), (4, 256, 1536), None, eighth, quarter, eighth, quarter, half, row, row,
        pair, pair, row, row, (1153, 32, 128), (2, 4, 16, 16, 512), (2, 8, 16, 16, 256), (2, 4, 72, 16, 128),
        (4, 72, 16, 128), (4, 72, 16, 128), (4, 72, 16, 128),
    ]
    return pl.pallas_call(
        backward,
        out_shape=(sds(*row), sds(288, 16, 128), sds(288, 16, 128), sds(8, 16, 16, 1536), sds(4, 16, 16, 3072)),
        in_specs=[SMEM] * 4 + [VMEM] * 3 + [ANY] * 2,
        out_specs=(VMEM, VMEM, VMEM, ANY, ANY),
        scratch_shapes=[
            *[pltpu.VMEM(shape, BF) if shape else pltpu.VMEM((256, 256), F32) for shape in shapes],
            pltpu.SemaphoreType.DMA((80,)),
            pltpu.SemaphoreType.DMA((80,)),
            pltpu.SemaphoreType.DMA((4,)),
            pltpu.SemaphoreType.DMA((2,)),
        ],
        compiler_params=pltpu.CompilerParams(collective_id=1, has_side_effects=True, vmem_limit_bytes=60 * MIB),
    )(table_one, table_two, tile_one, tile_two, inputs, out_grad, hidden_pre, first_blocks, second_blocks)[:3]


def solution(mesh):
    rows = P(("seq", "tensor"), None)
    cube = P("tensor", None, None)
    flat = P("tensor")
    in_specs = (rows, rows, P("seq", "tensor"), cube, flat, flat, flat, cube, flat, flat, flat)
    out_specs = (rows, P("tensor", "seq", None), P("tensor", "seq", None))
    return jax.shard_map(shards, mesh=mesh, in_specs=in_specs, out_specs=out_specs, check_vma=False)
```

```python
import jax
import jax.numpy as jnp
from jax import lax
from jax.experimental import pallas as pl
from jax.experimental.pallas import tpu as pltpu
from jax.sharding import PartitionSpec as P

MESH = pl.DeviceIdType.MESH
BF = jnp.bfloat16
F32 = jnp.float32
ANY = pl.BlockSpec(memory_space=pl.ANY)
SMEM = pl.BlockSpec(memory_space=pltpu.SMEM)
VMEM = pl.BlockSpec(memory_space=pltpu.VMEM)
MIB = 1024 * 1024

slope_coef = 0.7978845608028654
cubic_coef = 0.044715


def gelu_value(p):
    th = jnp.tanh(slope_coef * (p + cubic_coef * p * p * p))
    return 0.5 * p * (1.0 + th)


def gelu_slope(p):
    th = jnp.tanh(slope_coef * (p + cubic_coef * p * p * p))
    return 0.5 * (1.0 + th) + 0.5 * p * (1.0 - th * th) * slope_coef * (1.0 + 3.0 * cubic_coef * p * p)


class Here:
    def __init__(self):
        s = lax.axis_index("seq")
        t = lax.axis_index("tensor")
        self.s, self.t = s, t
        self.x, self.yl = s // 2, s % 2
        self.z, self.yh, self.c = t // 4, (t // 2) % 2, t % 2

    def dev(self, dx=0, fl=0, dz=0, fh=0, fc=0):
        x = (self.x + dx) % 4
        z = (self.z + dz) % 4
        yl = (self.yl + fl) % 2
        yh = (self.yh + fh) % 2
        c = (self.c + fc) % 2
        return (x * 2 + yl, z * 4 + yh * 2 + c)


class Copies:
    def __init__(self, send, recv):
        self.send_sems, self.recv_sems = send, recv
        self.sent = []

    def send(self, i, src, dst, device):
        copy = pltpu.make_async_remote_copy(
            src_ref=src,
            dst_ref=dst,
            send_sem=self.send_sems.at[i],
            recv_sem=self.recv_sems.at[i],
            device_id=device,
            device_id_type=MESH,
        )
        copy.start()
        self.sent.append(copy)

    def arrived(self, i, dst, device):
        pltpu.make_async_remote_copy(
            src_ref=dst,
            dst_ref=dst,
            send_sem=self.send_sems.at[i],
            recv_sem=self.recv_sems.at[i],
            device_id=device,
            device_id_type=MESH,
        ).wait_recv()

    def drain(self, count=None):
        for copy in self.sent[:count]:
            copy.wait_send()
        self.sent = self.sent[len(self.sent[:count]) :]


def greet(devices):
    barrier = pltpu.get_barrier_semaphore()
    for device in devices:
        pl.semaphore_signal(barrier, inc=1, device_id=device, device_id_type=MESH)
    pl.semaphore_wait(barrier, len(devices))


class TensorGather:
    def __init__(self, me, copies, base, own, slot):
        self.me, self.k, self.b, self.own, self.slot = me, copies, base, own, slot

    def at(self, dz, fh, fc=0):
        me = self.me
        return self.slot(((me.z + dz) % 4) * 4 + ((me.yh + fh) % 2) * 2 + (me.c + fc) % 2)

    def start(self):
        me, k, b, mine = self.me, self.k, self.b, self.at(0, 0)
        k.send(b + 1, self.own, mine, me.dev(fh=1))
        k.send(b + 2, self.own, mine, me.dev(dz=1))
        k.send(b + 3, self.own, mine, me.dev(dz=-1))
        k.send(b + 0, self.own, mine, me.dev(fc=1))

    def spread(self):
        me, k, b = self.me, self.k, self.b
        core = me.dev(fc=1)
        got = self.at(0, 1)
        k.arrived(b + 1, got, me.dev(fh=1))
        k.send(b + 4, got, got, me.dev(dz=1))
        k.send(b + 5, got, got, me.dev(dz=-1))
        k.send(b + 8, got, got, core)
        got = self.at(-1, 0)
        k.arrived(b + 2, got, me.dev(dz=-1))
        k.send(b + 6, got, got, me.dev(dz=1))
        k.send(b + 9, got, got, core)
        got = self.at(1, 0)
        k.arrived(b + 3, got, me.dev(dz=1))
        k.send(b + 11, got, got, core)

    def middle(self):
        me, k, b = self.me, self.k, self.b
        core = me.dev(fc=1)
        got = self.at(1, 1)
        k.arrived(b + 5, got, me.dev(dz=1))
        k.send(b + 7, got, got, me.dev(dz=-1))
        k.send(b + 12, got, got, core)
        got = self.at(-1, 1)
        k.arrived(b + 4, got, me.dev(dz=-1))
        k.send(b + 10, got, got, core)

    def finish(self):
        me, k, b = self.me, self.k, self.b
        core = me.dev(fc=1)
        got = self.at(2, 0)
        k.arrived(b + 6, got, me.dev(dz=-1))
        k.send(b + 13, got, got, core)
        got = self.at(2, 1)
        k.arrived(b + 7, got, me.dev(dz=1))
        k.send(b + 14, got, got, core)
        for i, dz, fh in ((0, 0, 0), (8, 0, 1), (9, -1, 0), (10, -1, 1), (11, 1, 0), (12, 1, 1), (13, 2, 0), (14, 2, 1)):
            k.arrived(b + i, self.at(dz, fh, 1), core)


class RowGather:
    def __init__(self, me, copies, base, own, slots):
        self.me, self.k, self.b, self.own, self.slots = me, copies, base, own, slots
        self.half = own.shape[0] // 2

    def start(self):
        me, k, b = self.me, self.k, self.b
        k.send(b + 0, self.own, self.slots.at[me.x], me.dev(dx=1))
        k.send(b + 1, self.own, self.slots.at[me.x], me.dev(dx=-1))

    def spread(self):
        me, k, b, half = self.me, self.k, self.b, self.half
        left, right = (me.x + 3) % 4, (me.x + 1) % 4
        k.arrived(b + 0, self.slots.at[left], me.dev(dx=-1))
        part = self.slots.at[left, pl.ds(0, half)]
        k.send(b + 2, part, part, me.dev(dx=1))
        k.arrived(b + 1, self.slots.at[right], me.dev(dx=1))
        part = self.slots.at[right, pl.ds(half, half)]
        k.send(b + 3, part, part, me.dev(dx=-1))

    def finish(self):
        me, k, b, half = self.me, self.k, self.b, self.half
        far = (me.x + 2) % 4
        k.arrived(b + 2, self.slots.at[far, pl.ds(0, half)], me.dev(dx=-1))
        k.arrived(b + 3, self.slots.at[far, pl.ds(half, half)], me.dev(dx=1))


class SeqGather:
    def __init__(self, me, copies, base, slots):
        self.me, self.k, self.b, self.slots = me, copies, base, slots

    def at(self, dx, fl):
        me = self.me
        return self.slots.at[(me.x + dx) % 4 * 2 + (me.yl + fl) % 2]

    def half(self, dx, fl, i):
        me = self.me
        return self.slots.at[(me.x + dx) % 4 * 2 + (me.yl + fl) % 2, pl.ds(i * 128, 128)]

    def start(self):
        me, k, b = self.me, self.k, self.b
        own = self.at(0, 0)
        k.send(b + 2, own, own, me.dev(fl=1))
        k.send(b + 0, own, own, me.dev(dx=1))
        k.send(b + 1, own, own, me.dev(dx=-1))

    def spread(self):
        me, k, b = self.me, self.k, self.b
        k.arrived(b + 0, self.at(-1, 0), me.dev(dx=-1))
        part = self.half(-1, 0, 0)
        k.send(b + 3, part, part, me.dev(dx=1))
        k.arrived(b + 1, self.at(1, 0), me.dev(dx=1))
        part = self.half(1, 0, 1)
        k.send(b + 4, part, part, me.dev(dx=-1))
        got = self.at(0, 1)
        k.arrived(b + 2, got, me.dev(fl=1))
        k.send(b + 5, got, got, me.dev(dx=1))
        k.send(b + 6, got, got, me.dev(dx=-1))

    def cross(self):
        me, k, b = self.me, self.k, self.b
        k.arrived(b + 5, self.at(-1, 1), me.dev(dx=-1))
        part = self.half(-1, 1, 0)
        k.send(b + 7, part, part, me.dev(dx=1))
        k.arrived(b + 6, self.at(1, 1), me.dev(dx=1))
        part = self.half(1, 1, 1)
        k.send(b + 8, part, part, me.dev(dx=-1))

    def finish(self):
        me, k, b = self.me, self.k, self.b
        for i, fl in ((3, 0), (7, 1)):
            k.arrived(b + i, self.half(2, fl, 0), me.dev(dx=-1))
            k.arrived(b + i + 1, self.half(2, fl, 1), me.dev(dx=1))


def blocks_at(blocks, table, rows, cols, width):
    return jnp.concatenate(
        [jnp.concatenate([blocks[table[r * width + j]] for j in cols], axis=1) for r in rows], axis=0
    )


NT = (((1,), (1,)), ((), ()))
TN = (((0,), (0,)), ((), ()))


def backward(
    table_one, table_two, tile_one, tile_two, inputs, grad, hidden, blocks_one, blocks_two,
    out, first, second, in_all, grad_all,
    rows, held, all_pre, all_acts, acc, in_cut, grad_cut, in_x, grad_x, mate, far_up, far_down, near_up, near_down, last,
    last_out, dense, lefts, in_lefts, two, two_got, two_sum, two_all, send, recv, local, chunk_sems,
):
    me = Here()
    greet([me.dev(fc=1), me.dev(fh=1), me.dev(dz=1), me.dev(dz=-1), me.dev(fl=1), me.dev(dx=1), me.dev(dx=-1), me.dev(dx=2)] + [me.dev(dx=dx, fl=1) for dx in (1, 2, 3)])
    k = Copies(send, recv)
    core, across, side = me.dev(fc=1), me.dev(fh=1), me.dev(fl=1)
    whole = TensorGather(me, k, 0, grad, lambda t: rows.at[t])
    grads = TensorGather(me, k, 15, grad_x, lambda t: grad_all.at[:, t])
    ins = TensorGather(me, k, 30, in_x, lambda t: in_all.at[:, t])
    pre_cols = SeqGather(me, k, 45, all_pre)
    act_cols = RowGather(me, k, 80, all_acts.at[me.x], all_acts)
    whole.start()
    rows[me.t] = grad[...]
    loads = [
        pltpu.make_async_copy(blocks, held.at[pl.ds(0, blocks.shape[0])], local.at[i])
        for i, blocks in enumerate((blocks_two, blocks_one))
    ]
    loads[0].start()
    held[blocks_two.shape[0]] = jnp.zeros(held.shape[1:], held.dtype)
    dense[dense.shape[0] - 1] = jnp.zeros(dense.shape[1:], dense.dtype)

    def cut(source, parts, n):
        wide, thin = n * 128, 128 // n

        def step(g, _):
            got = source[:, pl.ds(pl.multiple_of(g * wide, wide), wide)].astype(F32)
            for a in range(n):
                part = jnp.concatenate([got[:, q * 128 + a * thin : q * 128 + a * thin + thin] for q in range(n)], axis=1)
                parts[a, :, pl.ds(pl.multiple_of(g * 128, 128), 128)] = part.astype(BF)
            return 0

        lax.fori_loop(0, 96 // n, step, 0)

    cut(grad, grad_cut, 4)
    for dx in (1, 2, 3):
        k.send(56 + dx, grad_cut.at[(me.x + dx) % 4], grad_x.at[me.x], me.dev(dx=dx))
    grad_x[me.x] = grad_cut[me.x]

    def act(i, _):
        span = pl.ds(pl.multiple_of(i * 16, 16), 16)
        all_acts[me.x, span] = gelu_value(hidden[span].astype(F32)).astype(BF)
        return 0

    lax.fori_loop(0, 16, act, 0)
    act_cols.start()
    whole.spread()
    cut(inputs, in_cut, 8)
    others = [(dx, fl) for dx in range(4) for fl in range(2)][1:]
    for i, (dx, fl) in enumerate(others):
        to = (me.x + dx) % 4 * 2 + (me.yl + fl) % 2
        k.send(60 + i, in_cut.at[to], in_x.at[me.s], me.dev(dx=dx, fl=fl))
    in_x[me.s] = in_cut[me.s]
    whole.middle()
    for dx in (1, 2, 3):
        k.arrived(56 + dx, grad_x.at[(me.x + 4 - dx) % 4], me.dev(dx=-dx))
    grads.start()
    mine = [
        pltpu.make_async_copy(grad_x, grad_all.at[:, me.t], local.at[2]),
        pltpu.make_async_copy(in_x, in_all.at[:, me.t], local.at[3]),
    ]
    mine[0].start()
    act_cols.spread()
    whole.finish()
    settled = len(k.sent)
    loads[0].wait()

    def pre(n, _):
        acc[...] = jnp.zeros_like(acc)

        def step(i, _):
            j = i * 16
            w = blocks_at(held, table_two, (2 * n, 2 * n + 1), [j + a for a in range(16)], 96)
            left = rows[:, :, pl.ds(pl.multiple_of(j * 128, 2048), 2048)].reshape(256, 2048)
            acc[...] += lax.dot_general(left, w, NT, preferred_element_type=F32)
            return 0

        lax.fori_loop(0, 6, step, 0)
        span = pl.ds(pl.multiple_of(n * 256, 256), 256)
        all_pre[me.s, :, span] = (acc[...] * gelu_slope(hidden[:, span].astype(F32))).astype(BF)
        return 0

    lax.fori_loop(0, 2, pre, 0)
    grads.spread()
    lax.fori_loop(2, 4, pre, 0)
    for i, (dx, fl) in enumerate(others):
        k.arrived(60 + i, in_x.at[(me.x + 4 - dx) % 4 * 2 + (me.yl + fl) % 2], me.dev(dx=-dx, fl=fl))
    mine[1].start()
    grads.middle()
    ins.start()
    lax.fori_loop(4, 6, pre, 0)
    pre_cols.start()
    loads[1].start()

    def block_products(source, buffers, right, cuts, first_step, last_step):
        tall, wide = cuts * 256, 2048 // cuts
        thin = wide // 16

        def fetch(i):
            return pltpu.make_async_copy(
                source.at[:, :, :, pl.ds(pl.multiple_of(i * wide, wide), wide)], buffers.at[i % 2], chunk_sems.at[i % 2]
            )

        if first_step == 0:
            fetch(0).start()

        def step(i, _):
            @pl.when(i < 5)
            def _():
                fetch(i + 1).start()

            fetch(i).wait()
            got = lax.dot_general(
                buffers[i % 2].reshape(tall, wide), right[...].reshape(tall, 1536), TN, preferred_element_type=F32
            ).astype(BF)
            for a in range(16):
                for h in range(12):
                    dense[(i * 16 + a) * 12 + h, :thin] = got[a * thin : a * thin + thin, h * 128 : h * 128 + 128]
            return 0

        lax.fori_loop(first_step, last_step, step, 0)

    grads.finish()
    act_cols.finish()
    mine[0].wait()
    block_products(grad_all, lefts, all_acts, 4, 0, 3)
    ins.spread()
    block_products(grad_all, lefts, all_acts, 4, 3, 6)

    def cut_two(g, _):
        tiles = [dense[tile_two[g * 4 + q]].astype(F32) for q in range(4)]
        turned = jnp.concatenate(tiles, axis=0).T.astype(BF)
        for s in range(8):
            two[s % 2, s // 2, g] = turned[s * 16 : s * 16 + 16]
        return 0

    lax.fori_loop(0, 72, cut_two, 0)
    k.send(73, two.at[(me.yl + 1) % 2], two_got, side)
    pre_cols.spread()
    ins.middle()
    loads[1].wait()
    k.drain(settled)

    def back(q):
        def step(i, _):
            j = q * 24 + i * 4
            w = blocks_at(held, table_one, [j + a for a in range(4)], list(range(12)), 12)
            got = lax.dot_general(all_pre[me.s], w, NT, preferred_element_type=F32).astype(BF)
            for r in range(16):
                rows[r % 2 * 8 + r // 2, :, pl.ds(pl.multiple_of(j * 128, 512), 512)] = got[r * 16 : r * 16 + 16]
            return 0

        lax.fori_loop(0, 6, step, 0)
        span = pl.ds(q * 3072, 3072)
        k.send(67 + q, rows.at[pl.ds((me.c + 1) % 2 * 8, 8), :, span], mate.at[:, :, span], core)

    back(0)
    back(1)
    back(2)
    back(3)
    own = rows.at[pl.ds(me.c * 8, 8)]

    def add_pair(i, _):
        own[i] = (own[i].astype(F32) + mate[i].astype(F32)).astype(BF)
        return 0

    for q in range(4):
        k.arrived(67 + q, mate.at[:, :, pl.ds(q * 3072, 3072)], core)
    z2, zu, zd = (me.z + 2) % 4, (me.z + 1) % 4, (me.z + 3) % 4
    lax.fori_loop(z2 * 2, z2 * 2 + 2, add_pair, 0)
    k.send(71, own.at[z2 * 2], far_up, me.dev(dz=1))
    k.send(72, own.at[z2 * 2 + 1], far_down, me.dev(dz=-1))
    lax.fori_loop(zu * 2, zu * 2 + 2, add_pair, 0)
    lax.fori_loop(zd * 2, zd * 2 + 2, add_pair, 0)
    lax.fori_loop(me.z * 2, me.z * 2 + 2, add_pair, 0)

    ins.finish()
    pre_cols.cross()
    k.arrived(71, far_up, me.dev(dz=-1))
    own[zu * 2] = (own[zu * 2].astype(F32) + far_up[...].astype(F32)).astype(BF)
    k.send(74, own.at[pl.ds(zu * 2, 2)], near_up, me.dev(dz=1))
    k.arrived(72, far_down, me.dev(dz=1))
    own[zd * 2 + 1] = (own[zd * 2 + 1].astype(F32) + far_down[...].astype(F32)).astype(BF)
    k.send(75, own.at[pl.ds(zd * 2, 2)], near_down, me.dev(dz=-1))

    pre_cols.finish()
    mine[1].wait()
    block_products(in_all, in_lefts, all_pre, 8, 0, 3)

    k.arrived(73, two_got, side)
    for dx in (2, 1, 3, 0):
        to = (me.x + dx) % 4

        def add_two(g, _):
            two_sum[to, g] = (two[me.yl, to, g].astype(F32) + two_got[to, g].astype(F32)).astype(BF)
            return 0

        lax.fori_loop(0, 72, add_two, 0)
        if dx:
            k.send(76 + dx, two_sum.at[to], two_all.at[me.x], me.dev(dx=dx))
        else:
            two_all[me.x] = two_sum[me.x]

    block_products(in_all, in_lefts, all_pre, 8, 3, 6)

    k.arrived(74, near_up, me.dev(dz=-1))
    k.arrived(75, near_down, me.dev(dz=1))

    def add_three(h):
        return own[me.z * 2 + h].astype(F32) + near_up[h].astype(F32) + near_down[h].astype(F32)

    last_out[...] = add_three((me.yh + 1) % 2).astype(BF)
    k.send(76, last_out, last, across)

    def cut_one(g, _):
        for q in range(4):
            first[g * 4 + q] = dense[tile_one[g * 4 + q]][:16]
        return 0

    lax.fori_loop(0, 72, cut_one, 0)
    for dx in (1, 2, 3):
        k.arrived(76 + dx, two_all.at[(me.x + 4 - dx) % 4], me.dev(dx=-dx))

    def turn(g, _):
        for q in range(4):
            second[g * 4 + q] = jnp.concatenate([two_all[a, g][:, q * 32 : q * 32 + 32] for a in range(4)], axis=1)
        return 0

    lax.fori_loop(0, 72, turn, 0)
    k.arrived(76, last, across)
    out[...] = (add_three(me.yh) + last[...].astype(F32)).astype(BF)
    k.drain()


def sds(*shape):
    return jax.ShapeDtypeStruct(shape, BF)


def shards(inputs, out_grad, hidden_pre, first_blocks, first_feat, first_hid, first_live, second_blocks, second_feat, second_hid, second_live):
    base = lax.axis_index("tensor") * 12
    hid_one, hid_two = first_hid - base, second_hid - base
    slots = jnp.arange(288, dtype=jnp.int32)
    cells = jnp.arange(1152, dtype=jnp.int32)
    cell_one = jnp.where(slots < first_live[0], first_feat * 12 + hid_one, -1)
    cell_two = jnp.where(slots < second_live[0], hid_two * 96 + second_feat, -1)
    table_one = jnp.min(jnp.where(cells[:, None] == cell_one[None], slots[None], 288), axis=1)
    table_two = jnp.min(jnp.where(cells[:, None] == cell_two[None], slots[None], 288), axis=1)
    tile_one = jnp.where(slots < first_live[0], first_feat * 12 + hid_one, 1152)
    tile_two = jnp.where(slots < second_live[0], second_feat * 12 + hid_two, 1152)
    row, pair, half, quarter, eighth = (16, 12288), (2, 16, 12288), (8, 16, 12288), (4, 16, 3072), (8, 16, 1536)
    shapes = [
        (16, 16, 12288), (289, 128, 128), (8, 256, 1536), (4, 256, 1536), None, eighth, quarter, eighth, quarter, half, row, row,
        pair, pair, row, row, (1153, 32, 128), (2, 4, 16, 16, 512), (2, 8, 16, 16, 256), (2, 4, 72, 16, 128),
        (4, 72, 16, 128), (4, 72, 16, 128), (4, 72, 16, 128),
    ]
    return pl.pallas_call(
        backward,
        out_shape=(sds(*row), sds(288, 16, 128), sds(288, 16, 128), sds(8, 16, 16, 1536), sds(4, 16, 16, 3072)),
        in_specs=[SMEM] * 4 + [VMEM] * 3 + [ANY] * 2,
        out_specs=(VMEM, VMEM, VMEM, ANY, ANY),
        scratch_shapes=[
            *[pltpu.VMEM(shape, BF) if shape else pltpu.VMEM((256, 256), F32) for shape in shapes],
            pltpu.SemaphoreType.DMA((84,)),
            pltpu.SemaphoreType.DMA((84,)),
            pltpu.SemaphoreType.DMA((4,)),
            pltpu.SemaphoreType.DMA((2,)),
        ],
        compiler_params=pltpu.CompilerParams(collective_id=1, has_side_effects=True, vmem_limit_bytes=60 * MIB),
    )(table_one, table_two, tile_one, tile_two, inputs, out_grad, hidden_pre, first_blocks, second_blocks)[:3]


def solution(mesh):
    rows = P(("seq", "tensor"), None)
    cube = P("tensor", None, None)
    flat = P("tensor")
    in_specs = (rows, rows, P("seq", "tensor"), cube, flat, flat, flat, cube, flat, flat, flat)
    out_specs = (rows, P("tensor", "seq", None), P("tensor", "seq", None))
    return jax.shard_map(shards, mesh=mesh, in_specs=in_specs, out_specs=out_specs, check_vma=False)
```

```python
import jax
import jax.numpy as jnp
from jax import lax
from jax.experimental import pallas as pl
from jax.experimental.pallas import tpu as pltpu
from jax.sharding import PartitionSpec as P

MESH = pl.DeviceIdType.MESH
BF = jnp.bfloat16
F32 = jnp.float32
ANY = pl.BlockSpec(memory_space=pl.ANY)
SMEM = pl.BlockSpec(memory_space=pltpu.SMEM)
VMEM = pl.BlockSpec(memory_space=pltpu.VMEM)
MIB = 1024 * 1024

slope_coef = 0.7978845608028654
cubic_coef = 0.044715


def gelu_value(p):
    th = jnp.tanh(slope_coef * (p + cubic_coef * p * p * p))
    return 0.5 * p * (1.0 + th)


def gelu_slope(p):
    th = jnp.tanh(slope_coef * (p + cubic_coef * p * p * p))
    return 0.5 * (1.0 + th) + 0.5 * p * (1.0 - th * th) * slope_coef * (1.0 + 3.0 * cubic_coef * p * p)


class Here:
    def __init__(self):
        s = lax.axis_index("seq")
        t = lax.axis_index("tensor")
        self.s, self.t = s, t
        self.x, self.yl = s // 2, s % 2
        self.z, self.yh, self.c = t // 4, (t // 2) % 2, t % 2

    def dev(self, dx=0, fl=0, dz=0, fh=0, fc=0):
        x = (self.x + dx) % 4
        z = (self.z + dz) % 4
        yl = (self.yl + fl) % 2
        yh = (self.yh + fh) % 2
        c = (self.c + fc) % 2
        return (x * 2 + yl, z * 4 + yh * 2 + c)


class Copies:
    def __init__(self, send, recv):
        self.send_sems, self.recv_sems = send, recv
        self.sent = []

    def send(self, i, src, dst, device):
        copy = pltpu.make_async_remote_copy(
            src_ref=src,
            dst_ref=dst,
            send_sem=self.send_sems.at[i],
            recv_sem=self.recv_sems.at[i],
            device_id=device,
            device_id_type=MESH,
        )
        copy.start()
        self.sent.append(copy)

    def arrived(self, i, dst, device):
        pltpu.make_async_remote_copy(
            src_ref=dst,
            dst_ref=dst,
            send_sem=self.send_sems.at[i],
            recv_sem=self.recv_sems.at[i],
            device_id=device,
            device_id_type=MESH,
        ).wait_recv()

    def drain(self, count=None):
        for copy in self.sent[:count]:
            copy.wait_send()
        self.sent = self.sent[len(self.sent[:count]) :]


def greet(devices):
    barrier = pltpu.get_barrier_semaphore()
    for device in devices:
        pl.semaphore_signal(barrier, inc=1, device_id=device, device_id_type=MESH)
    pl.semaphore_wait(barrier, len(devices))


class TensorGather:
    def __init__(self, me, copies, base, own, slot):
        self.me, self.k, self.b, self.own, self.slot = me, copies, base, own, slot

    def at(self, dz, fh, fc=0):
        me = self.me
        return self.slot(((me.z + dz) % 4) * 4 + ((me.yh + fh) % 2) * 2 + (me.c + fc) % 2)

    def start(self):
        me, k, b, mine = self.me, self.k, self.b, self.at(0, 0)
        k.send(b + 1, self.own, mine, me.dev(fh=1))
        k.send(b + 2, self.own, mine, me.dev(dz=1))
        k.send(b + 3, self.own, mine, me.dev(dz=-1))
        k.send(b + 0, self.own, mine, me.dev(fc=1))

    def spread(self):
        me, k, b = self.me, self.k, self.b
        core = me.dev(fc=1)
        got = self.at(0, 1)
        k.arrived(b + 1, got, me.dev(fh=1))
        k.send(b + 4, got, got, me.dev(dz=1))
        k.send(b + 5, got, got, me.dev(dz=-1))
        k.send(b + 8, got, got, core)
        got = self.at(-1, 0)
        k.arrived(b + 2, got, me.dev(dz=-1))
        k.send(b + 6, got, got, me.dev(dz=1))
        k.send(b + 9, got, got, core)
        got = self.at(1, 0)
        k.arrived(b + 3, got, me.dev(dz=1))
        k.send(b + 11, got, got, core)

    def middle(self):
        me, k, b = self.me, self.k, self.b
        core = me.dev(fc=1)
        got = self.at(1, 1)
        k.arrived(b + 5, got, me.dev(dz=1))
        k.send(b + 7, got, got, me.dev(dz=-1))
        k.send(b + 12, got, got, core)
        got = self.at(-1, 1)
        k.arrived(b + 4, got, me.dev(dz=-1))
        k.send(b + 10, got, got, core)

    def finish(self):
        me, k, b = self.me, self.k, self.b
        core = me.dev(fc=1)
        got = self.at(2, 0)
        k.arrived(b + 6, got, me.dev(dz=-1))
        k.send(b + 13, got, got, core)
        got = self.at(2, 1)
        k.arrived(b + 7, got, me.dev(dz=1))
        k.send(b + 14, got, got, core)
        for i, dz, fh in ((0, 0, 0), (8, 0, 1), (9, -1, 0), (10, -1, 1), (11, 1, 0), (12, 1, 1), (13, 2, 0), (14, 2, 1)):
            k.arrived(b + i, self.at(dz, fh, 1), core)


class RowGather:
    def __init__(self, me, copies, base, own, slots):
        self.me, self.k, self.b, self.own, self.slots = me, copies, base, own, slots
        self.half = own.shape[0] // 2

    def start(self):
        me, k, b = self.me, self.k, self.b
        k.send(b + 0, self.own, self.slots.at[me.x], me.dev(dx=1))
        k.send(b + 1, self.own, self.slots.at[me.x], me.dev(dx=-1))

    def spread(self):
        me, k, b, half = self.me, self.k, self.b, self.half
        left, right = (me.x + 3) % 4, (me.x + 1) % 4
        k.arrived(b + 0, self.slots.at[left], me.dev(dx=-1))
        part = self.slots.at[left, pl.ds(0, half)]
        k.send(b + 2, part, part, me.dev(dx=1))
        k.arrived(b + 1, self.slots.at[right], me.dev(dx=1))
        part = self.slots.at[right, pl.ds(half, half)]
        k.send(b + 3, part, part, me.dev(dx=-1))

    def finish(self):
        me, k, b, half = self.me, self.k, self.b, self.half
        far = (me.x + 2) % 4
        k.arrived(b + 2, self.slots.at[far, pl.ds(0, half)], me.dev(dx=-1))
        k.arrived(b + 3, self.slots.at[far, pl.ds(half, half)], me.dev(dx=1))


class SeqGather:
    def __init__(self, me, copies, base, slots, first, last):
        self.me, self.k, self.b, self.slots = me, copies, base, slots
        self.span = pl.ds(first, last - first)

    def at(self, dx, fl):
        me = self.me
        return self.slots.at[(me.x + dx) % 4 * 2 + (me.yl + fl) % 2, :, self.span]

    def half(self, dx, fl, i):
        me = self.me
        return self.slots.at[(me.x + dx) % 4 * 2 + (me.yl + fl) % 2, pl.ds(i * 128, 128), self.span]

    def start(self):
        me, k, b = self.me, self.k, self.b
        own = self.at(0, 0)
        k.send(b + 2, own, own, me.dev(fl=1))
        k.send(b + 0, own, own, me.dev(dx=1))
        k.send(b + 1, own, own, me.dev(dx=-1))

    def spread(self):
        me, k, b = self.me, self.k, self.b
        k.arrived(b + 0, self.at(-1, 0), me.dev(dx=-1))
        part = self.half(-1, 0, 0)
        k.send(b + 3, part, part, me.dev(dx=1))
        k.arrived(b + 1, self.at(1, 0), me.dev(dx=1))
        part = self.half(1, 0, 1)
        k.send(b + 4, part, part, me.dev(dx=-1))
        got = self.at(0, 1)
        k.arrived(b + 2, got, me.dev(fl=1))
        k.send(b + 5, got, got, me.dev(dx=1))
        k.send(b + 6, got, got, me.dev(dx=-1))

    def cross(self):
        me, k, b = self.me, self.k, self.b
        k.arrived(b + 5, self.at(-1, 1), me.dev(dx=-1))
        part = self.half(-1, 1, 0)
        k.send(b + 7, part, part, me.dev(dx=1))
        k.arrived(b + 6, self.at(1, 1), me.dev(dx=1))
        part = self.half(1, 1, 1)
        k.send(b + 8, part, part, me.dev(dx=-1))

    def finish(self):
        me, k, b = self.me, self.k, self.b
        for i, fl in ((3, 0), (7, 1)):
            k.arrived(b + i, self.half(2, fl, 0), me.dev(dx=-1))
            k.arrived(b + i + 1, self.half(2, fl, 1), me.dev(dx=1))


def blocks_at(blocks, table, rows, cols, width):
    return jnp.concatenate(
        [jnp.concatenate([blocks[table[r * width + j]] for j in cols], axis=1) for r in rows], axis=0
    )


NT = (((1,), (1,)), ((), ()))
TN = (((0,), (0,)), ((), ()))


def backward(
    table_one, table_two, tile_one, tile_two, inputs, grad, hidden, blocks_one, blocks_two,
    out, first, second, in_all, grad_all,
    rows, held, all_pre, all_acts, acc, in_cut, grad_cut, in_x, grad_x, mate, far_up, far_down, near_up, near_down, last,
    last_out, dense, lefts, in_lefts, two, two_got, two_sum, two_all, send, recv, local, chunk_sems,
):
    me = Here()
    greet([me.dev(fc=1), me.dev(fh=1), me.dev(dz=1), me.dev(dz=-1), me.dev(fl=1), me.dev(dx=1), me.dev(dx=-1), me.dev(dx=2)] + [me.dev(dx=dx, fl=1) for dx in (1, 2, 3)])
    k = Copies(send, recv)
    core, across, side = me.dev(fc=1), me.dev(fh=1), me.dev(fl=1)
    whole = TensorGather(me, k, 0, grad, lambda t: rows.at[t])
    grads = TensorGather(me, k, 15, grad_x, lambda t: grad_all.at[:, t])
    ins = TensorGather(me, k, 30, in_x, lambda t: in_all.at[:, t])
    pre_cols = SeqGather(me, k, 45, all_pre, 0, 1024)
    end_cols = SeqGather(me, k, 84, all_pre, 1024, 1536)
    act_cols = RowGather(me, k, 80, all_acts.at[me.x], all_acts)
    whole.start()
    rows[me.t] = grad[...]
    loads = [
        pltpu.make_async_copy(blocks, held.at[pl.ds(0, blocks.shape[0])], local.at[i])
        for i, blocks in enumerate((blocks_two, blocks_one))
    ]
    loads[0].start()
    held[blocks_two.shape[0]] = jnp.zeros(held.shape[1:], held.dtype)
    dense[dense.shape[0] - 1] = jnp.zeros(dense.shape[1:], dense.dtype)

    def cut(source, parts, n):
        wide, thin = n * 128, 128 // n

        def step(g, _):
            got = source[:, pl.ds(pl.multiple_of(g * wide, wide), wide)].astype(F32)
            for a in range(n):
                part = jnp.concatenate([got[:, q * 128 + a * thin : q * 128 + a * thin + thin] for q in range(n)], axis=1)
                parts[a, :, pl.ds(pl.multiple_of(g * 128, 128), 128)] = part.astype(BF)
            return 0

        lax.fori_loop(0, 96 // n, step, 0)

    cut(grad, grad_cut, 4)
    for dx in (1, 2, 3):
        k.send(56 + dx, grad_cut.at[(me.x + dx) % 4], grad_x.at[me.x], me.dev(dx=dx))
    grad_x[me.x] = grad_cut[me.x]

    def act(i, _):
        span = pl.ds(pl.multiple_of(i * 16, 16), 16)
        all_acts[me.x, span] = gelu_value(hidden[span].astype(F32)).astype(BF)
        return 0

    lax.fori_loop(0, 16, act, 0)
    act_cols.start()
    whole.spread()
    cut(inputs, in_cut, 8)
    others = [(dx, fl) for dx in range(4) for fl in range(2)][1:]
    for i, (dx, fl) in enumerate(others):
        to = (me.x + dx) % 4 * 2 + (me.yl + fl) % 2
        k.send(60 + i, in_cut.at[to], in_x.at[me.s], me.dev(dx=dx, fl=fl))
    in_x[me.s] = in_cut[me.s]
    whole.middle()
    for dx in (1, 2, 3):
        k.arrived(56 + dx, grad_x.at[(me.x + 4 - dx) % 4], me.dev(dx=-dx))
    grads.start()
    mine = [
        pltpu.make_async_copy(grad_x, grad_all.at[:, me.t], local.at[2]),
        pltpu.make_async_copy(in_x, in_all.at[:, me.t], local.at[3]),
    ]
    mine[0].start()
    act_cols.spread()
    whole.finish()
    settled = len(k.sent)
    loads[0].wait()

    def pre(n, _):
        acc[...] = jnp.zeros_like(acc)

        def step(i, _):
            j = i * 16
            w = blocks_at(held, table_two, (2 * n, 2 * n + 1), [j + a for a in range(16)], 96)
            left = rows[:, :, pl.ds(pl.multiple_of(j * 128, 2048), 2048)].reshape(256, 2048)
            acc[...] += lax.dot_general(left, w, NT, preferred_element_type=F32)
            return 0

        lax.fori_loop(0, 6, step, 0)
        span = pl.ds(pl.multiple_of(n * 256, 256), 256)
        all_pre[me.s, :, span] = (acc[...] * gelu_slope(hidden[:, span].astype(F32))).astype(BF)
        return 0

    lax.fori_loop(0, 2, pre, 0)
    grads.spread()
    lax.fori_loop(2, 4, pre, 0)
    pre_cols.start()
    for i, (dx, fl) in enumerate(others):
        k.arrived(60 + i, in_x.at[(me.x + 4 - dx) % 4 * 2 + (me.yl + fl) % 2], me.dev(dx=-dx, fl=fl))
    mine[1].start()
    grads.middle()
    ins.start()
    lax.fori_loop(4, 6, pre, 0)
    end_cols.start()
    loads[1].start()

    def block_products(source, buffers, right, cuts, first_step, last_step):
        tall, wide = cuts * 256, 2048 // cuts
        thin = wide // 16

        def fetch(i):
            return pltpu.make_async_copy(
                source.at[:, :, :, pl.ds(pl.multiple_of(i * wide, wide), wide)], buffers.at[i % 2], chunk_sems.at[i % 2]
            )

        if first_step == 0:
            fetch(0).start()

        def step(i, _):
            @pl.when(i < 5)
            def _():
                fetch(i + 1).start()

            fetch(i).wait()
            got = lax.dot_general(
                buffers[i % 2].reshape(tall, wide), right[...].reshape(tall, 1536), TN, preferred_element_type=F32
            ).astype(BF)
            for a in range(16):
                for h in range(12):
                    dense[(i * 16 + a) * 12 + h, :thin] = got[a * thin : a * thin + thin, h * 128 : h * 128 + 128]
            return 0

        lax.fori_loop(first_step, last_step, step, 0)

    grads.finish()
    act_cols.finish()
    mine[0].wait()
    block_products(grad_all, lefts, all_acts, 4, 0, 3)
    pre_cols.spread()
    ins.spread()
    block_products(grad_all, lefts, all_acts, 4, 3, 6)

    def cut_two(g, _):
        tiles = [dense[tile_two[g * 4 + q]].astype(F32) for q in range(4)]
        turned = jnp.concatenate(tiles, axis=0).T.astype(BF)
        for s in range(8):
            two[s % 2, s // 2, g] = turned[s * 16 : s * 16 + 16]
        return 0

    lax.fori_loop(0, 72, cut_two, 0)
    k.send(73, two.at[(me.yl + 1) % 2], two_got, side)
    end_cols.spread()
    ins.middle()
    loads[1].wait()
    k.drain(settled)

    def back(q):
        def step(i, _):
            j = q * 24 + i * 4
            w = blocks_at(held, table_one, [j + a for a in range(4)], list(range(12)), 12)
            got = lax.dot_general(all_pre[me.s], w, NT, preferred_element_type=F32).astype(BF)
            for r in range(16):
                rows[r % 2 * 8 + r // 2, :, pl.ds(pl.multiple_of(j * 128, 512), 512)] = got[r * 16 : r * 16 + 16]
            return 0

        lax.fori_loop(0, 6, step, 0)
        span = pl.ds(q * 3072, 3072)
        k.send(67 + q, rows.at[pl.ds((me.c + 1) % 2 * 8, 8), :, span], mate.at[:, :, span], core)

    back(0)
    back(1)
    pre_cols.cross()
    back(2)
    back(3)
    own = rows.at[pl.ds(me.c * 8, 8)]

    def add_pair(i, _):
        own[i] = (own[i].astype(F32) + mate[i].astype(F32)).astype(BF)
        return 0

    for q in range(4):
        k.arrived(67 + q, mate.at[:, :, pl.ds(q * 3072, 3072)], core)
    z2, zu, zd = (me.z + 2) % 4, (me.z + 1) % 4, (me.z + 3) % 4
    lax.fori_loop(z2 * 2, z2 * 2 + 2, add_pair, 0)
    k.send(71, own.at[z2 * 2], far_up, me.dev(dz=1))
    k.send(72, own.at[z2 * 2 + 1], far_down, me.dev(dz=-1))
    lax.fori_loop(zu * 2, zu * 2 + 2, add_pair, 0)
    lax.fori_loop(zd * 2, zd * 2 + 2, add_pair, 0)
    lax.fori_loop(me.z * 2, me.z * 2 + 2, add_pair, 0)

    ins.finish()
    end_cols.cross()
    k.arrived(71, far_up, me.dev(dz=-1))
    own[zu * 2] = (own[zu * 2].astype(F32) + far_up[...].astype(F32)).astype(BF)
    k.send(74, own.at[pl.ds(zu * 2, 2)], near_up, me.dev(dz=1))
    k.arrived(72, far_down, me.dev(dz=1))
    own[zd * 2 + 1] = (own[zd * 2 + 1].astype(F32) + far_down[...].astype(F32)).astype(BF)
    k.send(75, own.at[pl.ds(zd * 2, 2)], near_down, me.dev(dz=-1))

    pre_cols.finish()
    end_cols.finish()
    mine[1].wait()
    block_products(in_all, in_lefts, all_pre, 8, 0, 3)

    k.arrived(73, two_got, side)
    for dx in (2, 1, 3, 0):
        to = (me.x + dx) % 4

        def add_two(g, _):
            two_sum[to, g] = (two[me.yl, to, g].astype(F32) + two_got[to, g].astype(F32)).astype(BF)
            return 0

        lax.fori_loop(0, 72, add_two, 0)
        if dx:
            k.send(76 + dx, two_sum.at[to], two_all.at[me.x], me.dev(dx=dx))
        else:
            two_all[me.x] = two_sum[me.x]

    block_products(in_all, in_lefts, all_pre, 8, 3, 6)

    k.arrived(74, near_up, me.dev(dz=-1))
    k.arrived(75, near_down, me.dev(dz=1))

    def add_three(h):
        return own[me.z * 2 + h].astype(F32) + near_up[h].astype(F32) + near_down[h].astype(F32)

    last_out[...] = add_three((me.yh + 1) % 2).astype(BF)
    k.send(76, last_out, last, across)

    def cut_one(g, _):
        for q in range(4):
            first[g * 4 + q] = dense[tile_one[g * 4 + q]][:16]
        return 0

    lax.fori_loop(0, 72, cut_one, 0)
    for dx in (1, 2, 3):
        k.arrived(76 + dx, two_all.at[(me.x + 4 - dx) % 4], me.dev(dx=-dx))

    def turn(g, _):
        for q in range(4):
            second[g * 4 + q] = jnp.concatenate([two_all[a, g][:, q * 32 : q * 32 + 32] for a in range(4)], axis=1)
        return 0

    lax.fori_loop(0, 72, turn, 0)
    k.arrived(76, last, across)
    out[...] = (add_three(me.yh) + last[...].astype(F32)).astype(BF)
    k.drain()


def sds(*shape):
    return jax.ShapeDtypeStruct(shape, BF)


def shards(inputs, out_grad, hidden_pre, first_blocks, first_feat, first_hid, first_live, second_blocks, second_feat, second_hid, second_live):
    base = lax.axis_index("tensor") * 12
    hid_one, hid_two = first_hid - base, second_hid - base
    slots = jnp.arange(288, dtype=jnp.int32)
    cells = jnp.arange(1152, dtype=jnp.int32)
    cell_one = jnp.where(slots < first_live[0], first_feat * 12 + hid_one, -1)
    cell_two = jnp.where(slots < second_live[0], hid_two * 96 + second_feat, -1)
    table_one = jnp.min(jnp.where(cells[:, None] == cell_one[None], slots[None], 288), axis=1)
    table_two = jnp.min(jnp.where(cells[:, None] == cell_two[None], slots[None], 288), axis=1)
    tile_one = jnp.where(slots < first_live[0], first_feat * 12 + hid_one, 1152)
    tile_two = jnp.where(slots < second_live[0], second_feat * 12 + hid_two, 1152)
    row, pair, half, quarter, eighth = (16, 12288), (2, 16, 12288), (8, 16, 12288), (4, 16, 3072), (8, 16, 1536)
    shapes = [
        (16, 16, 12288), (289, 128, 128), (8, 256, 1536), (4, 256, 1536), None, eighth, quarter, eighth, quarter, half, row, row,
        pair, pair, row, row, (1153, 32, 128), (2, 4, 16, 16, 512), (2, 8, 16, 16, 256), (2, 4, 72, 16, 128),
        (4, 72, 16, 128), (4, 72, 16, 128), (4, 72, 16, 128),
    ]
    return pl.pallas_call(
        backward,
        out_shape=(sds(*row), sds(288, 16, 128), sds(288, 16, 128), sds(8, 16, 16, 1536), sds(4, 16, 16, 3072)),
        in_specs=[SMEM] * 4 + [VMEM] * 3 + [ANY] * 2,
        out_specs=(VMEM, VMEM, VMEM, ANY, ANY),
        scratch_shapes=[
            *[pltpu.VMEM(shape, BF) if shape else pltpu.VMEM((256, 256), F32) for shape in shapes],
            pltpu.SemaphoreType.DMA((93,)),
            pltpu.SemaphoreType.DMA((93,)),
            pltpu.SemaphoreType.DMA((4,)),
            pltpu.SemaphoreType.DMA((2,)),
        ],
        compiler_params=pltpu.CompilerParams(collective_id=1, has_side_effects=True, vmem_limit_bytes=60 * MIB),
    )(table_one, table_two, tile_one, tile_two, inputs, out_grad, hidden_pre, first_blocks, second_blocks)[:3]


def solution(mesh):
    rows = P(("seq", "tensor"), None)
    cube = P("tensor", None, None)
    flat = P("tensor")
    in_specs = (rows, rows, P("seq", "tensor"), cube, flat, flat, flat, cube, flat, flat, flat)
    out_specs = (rows, P("tensor", "seq", None), P("tensor", "seq", None))
    return jax.shard_map(shards, mesh=mesh, in_specs=in_specs, out_specs=out_specs, check_vma=False)
```
